128 devices in a mesh: view: 16 (over x, y), tok: 8 (over z, core).
Axes of the slice: x: 4, y: 4, z: 4, core: 2. Of those that a mesh axis runs over, the one named last changes fastest.
Arguments:
- x_target: bfloat16 [16, 4096, 1024], P('view', 'tok'), may hold values from -50 to 50
- cond_x: bfloat16 [2048, 1024], P(('view', 'tok')), may hold values from -50 to 50
- w_query: bfloat16 [1024, 1024], replicated, may hold values from -1 to 1
- w_key: bfloat16 [1024, 1024], replicated, may hold values from -1 to 1
- w_value: bfloat16 [1024, 1024], replicated, may hold values from -0.1875 to 0.1875
- w_out: bfloat16 [1024, 1024], replicated, may hold values from -0.1875 to 0.1875
- epi_lists: int32 [16, 32, 8, 2], P('view', 'tok'), may hold values from -1 to 31, as said below
Outputs:
- mixed: bfloat16 [16, 4096, 1024], P('view', 'tok')
The draws below stay inside these ranges and needn't reach their ends.
Inputs may be any that keep to these rules, and one draw needn't show every extreme that they name: `epi_lists`: each query block in row band t (blocks t * 4 onward) names only key blocks of bands t - 1, t, t + 1; pairs of one query block are distinct and its used entries come first. Over the query blocks of one band of one view, at most 2 distinct key blocks of any one view are named, and in every band of every view some view has exactly 2; one query block of each band names 8 pairs.
All inputs are finite; a program needn't handle non-finite values.
Results may differ from the reference program's by a relative error of at most 0.012.
Values may be sent and summed in bfloat16 or wider, within the bound.
A program may use at most 192 MiB of HBM per device.

```python
import math
import jax
import jax.numpy as jnp
from jax import lax

D = 1024
HD = 64
BLK = 128
MOST = 8
CAP = 2
TOK_DEV = 512
VIEWS = 16
VIEW_TOK = 4096
NB = 32
COND_TOK = 2048


def base_weight(key):
    return jax.random.normal(jax.random.fold_in(key, 101), (D, D), jnp.float32) / math.sqrt(D)


def draw_w_query(key, part):
    shared = base_weight(key)
    return shared.astype(jnp.bfloat16)


def draw_w_key(key, part):
    key = jax.random.fold_in(key, 2)
    own = jax.random.normal(key, (D, D), jnp.float32) / math.sqrt(D)
    mixed = own
    return mixed.astype(jnp.bfloat16)


def draw_cond_x(key, part):
    key = jax.random.fold_in(key, 3)
    first = jax.random.fold_in(key, 0)
    drawn = 2.0 * jnp.clip(jax.random.normal(first, (COND_TOK, D), jnp.float32), -6.0, 6.0)
    return drawn.astype(jnp.bfloat16)


def draw_x_target(key, part):
    key = jax.random.fold_in(key, 4)
    first = jax.random.fold_in(key, 0)
    total_rows = VIEWS * VIEW_TOK
    drawn = 2.0 * jnp.clip(jax.random.normal(first, (total_rows, D), jnp.float32), -6.0, 6.0)
    return drawn.reshape(VIEWS, VIEW_TOK, D).astype(jnp.bfloat16)


def draw_epi_lists(key, part):
    key = jax.random.fold_in(key, 7)
    keys = jax.random.split(key, 5)
    bands = VIEW_TOK // TOK_DEV
    per_band = TOK_DEV // BLK
    span = 3 * per_band
    pool = VIEWS * CAP
    band_ids = jnp.arange(bands)[None, :, None, None]
    global_block = (band_ids - 1) * per_band + jnp.arange(span)[None, None, None, :]
    inside = (global_block >= 0) & (global_block < NB)
    scores = jax.random.randint(keys[0], (VIEWS, bands, VIEWS, span), 0, 1 << 20) * 64 + jnp.arange(span)
    scores = jnp.where(inside, scores, -1)
    _, position = lax.top_k(scores, CAP)
    candidate = (band_ids - 1) * per_band + position
    pool_block = candidate.reshape(VIEWS, bands, pool)
    pool_view = jnp.broadcast_to(jnp.repeat(jnp.arange(VIEWS), CAP)[None, None, :], (VIEWS, bands, pool))
    counts = jax.random.randint(keys[1], (VIEWS, bands, per_band), 1, MOST + 1)
    forced_block = jax.random.randint(keys[2], (VIEWS, bands), 0, per_band)
    is_forced = jnp.arange(per_band)[None, None, :] == forced_block[..., None]
    counts = jnp.where(is_forced, MOST, counts)
    forced_view = jax.random.randint(keys[3], (VIEWS, bands), 0, VIEWS)
    order_scores = jax.random.randint(keys[4], (VIEWS, bands, per_band, pool), 0, 1 << 20) * 256 + jnp.arange(pool)
    boosted = (pool_view == forced_view[..., None])[:, :, None, :] & is_forced[..., None]
    order_scores = order_scores + jnp.where(boosted, 1 << 29, 0)
    _, order = lax.top_k(order_scores, MOST)
    chosen_view = jnp.take_along_axis(jnp.broadcast_to(pool_view[:, :, None, :], order_scores.shape), order, axis=-1)
    chosen_block = jnp.take_along_axis(jnp.broadcast_to(pool_block[:, :, None, :], order_scores.shape), order, axis=-1)
    keep = jnp.arange(MOST)[None, None, None, :] < counts[..., None]
    chosen_view = jnp.where(keep, chosen_view, -1)
    chosen_block = jnp.where(keep, chosen_block, -1)
    stacked = jnp.stack([chosen_view, chosen_block], axis=-1)
    return stacked.reshape(VIEWS, NB, MOST, 2).astype(jnp.int32)


def gaussian(rng, extent, spread, limit, kind=jnp.bfloat16):
    return jnp.clip(spread * jax.random.normal(rng, extent, jnp.float32), -limit, limit).astype(kind)


def setup_inputs(seed: int = 0) -> dict:
    streams_of = jax.random.split(jax.random.key(seed), 8)
    x_target = draw_x_target(jax.random.fold_in(streams_of[7], 71), 0)
    cond_x = draw_cond_x(jax.random.fold_in(streams_of[7], 71), 0)
    w_query = draw_w_query(jax.random.fold_in(streams_of[7], 71), 0)
    w_key = draw_w_key(jax.random.fold_in(streams_of[7], 71), 0)
    w_value = gaussian(streams_of[4], (D, D), D ** -0.5, 0.1875)
    w_out = gaussian(streams_of[5], (D, D), D ** -0.5, 0.1875)
    epi_lists = draw_epi_lists(jax.random.fold_in(streams_of[7], 71), 0)
    return dict(x_target=x_target, cond_x=cond_x, w_query=w_query, w_key=w_key, w_value=w_value, w_out=w_out, epi_lists=epi_lists)


def reference(x_target, cond_x, w_query, w_key, w_value, w_out, epi_lists):
    heads = D // HD
    flat = x_target.reshape(VIEWS * VIEW_TOK, D)
    query = jnp.dot(flat, w_query, preferred_element_type=jnp.float32).astype(jnp.bfloat16)
    keys_all = jnp.dot(flat, w_key, preferred_element_type=jnp.float32).astype(jnp.bfloat16)
    values_all = jnp.dot(flat, w_value, preferred_element_type=jnp.float32).astype(jnp.bfloat16)
    cond_keys = jnp.dot(cond_x, w_key, preferred_element_type=jnp.float32).astype(jnp.bfloat16)
    cond_values = jnp.dot(cond_x, w_value, preferred_element_type=jnp.float32).astype(jnp.bfloat16)
    key_blocks = keys_all.reshape(VIEWS * NB, BLK, D)
    value_blocks = values_all.reshape(VIEWS * NB, BLK, D)

    def one_block(index):
        index = index.astype(jnp.int32)
        view = index // NB
        qblock = index % NB
        rows = lax.dynamic_slice_in_dim(query, (index * BLK).astype(jnp.int32), BLK, 0)
        entries = epi_lists[view, qblock]
        valid = entries[:, 0] >= 0
        picks = (jnp.clip(entries[:, 0], 0) * NB + jnp.clip(entries[:, 1], 0)).astype(jnp.int32)
        epi_keys = key_blocks[picks].reshape(MOST * BLK, D)
        epi_values = value_blocks[picks].reshape(MOST * BLK, D)
        keyset = jnp.concatenate([cond_keys, epi_keys], axis=0)
        valueset = jnp.concatenate([cond_values, epi_values], axis=0)
        masking = jnp.where(jnp.repeat(valid, BLK), 0.0, -1e30).astype(jnp.float32)
        bias = jnp.concatenate([jnp.zeros((COND_TOK,), jnp.float32), masking])
        query_heads = rows.astype(jnp.float32).reshape(BLK, heads, HD)
        key_heads = keyset.astype(jnp.float32).reshape(-1, heads, HD)
        value_heads = valueset.astype(jnp.float32).reshape(-1, heads, HD)
        scores = jnp.einsum("qhd,khd->qhk", query_heads, key_heads) * (HD ** -0.5) + bias
        peak = jnp.max(scores, axis=-1, keepdims=True)
        weights = jnp.exp(scores - peak)
        total = jnp.sum(weights, axis=-1)
        rounded = lax.optimization_barrier(weights.astype(jnp.bfloat16)).astype(jnp.float32)
        attended = jnp.einsum("qhk,khd->qhd", rounded, value_heads) / total[..., None]
        return attended.reshape(BLK, D).astype(jnp.bfloat16)

    attended = lax.map(one_block, jnp.arange(VIEWS * NB, dtype=jnp.int32)).reshape(VIEWS * VIEW_TOK, D)
    mixed = jnp.dot(attended, w_out, preferred_element_type=jnp.float32).astype(jnp.bfloat16)
    return mixed.reshape(VIEWS, VIEW_TOK, D)
```

```python
import functools
import math

import jax
import jax.numpy as jnp
from jax import lax
from jax.experimental import pallas as pl
from jax.experimental.pallas import tpu as pltpu
from jax.sharding import PartitionSpec as P

HD = 64
BLK = 128
MESH = pl.DeviceIdType.MESH
LAG = 3


def dot(a, b):
    return jnp.dot(a, b, preferred_element_type=jnp.float32)


def dot_t(a, b):
    return lax.dot_general(a, b, (((1,), (1,)), ((), ())), preferred_element_type=jnp.float32)


def kernel(
    nview, ntok, rows, crows, most,
    x_hbm, cond_hbm, wq_hbm, wk_hbm, wv_hbm, wo_hbm, lists_hbm,
    out_hbm,
    xall, wq, wk, wv, wo,
    qsend, kvsend, csend, lsend,
    qrecv, pool, condkv, lists_v, lists_s,
    vcond, qpad, oacc, mrow, osend, orecv, att, outv,
    load_sem, q_ss, q_rs, kv_ss, kv_rs, c_ss, c_rs, l_ss, l_rs, g_ss, g_rs, f_ss, f_rs, o_ss, o_rs, smem_sem, out_sem,
):
    view = lax.axis_index("view")
    tok = lax.axis_index("tok")
    width = nview * HD
    half = rows // 2
    nblk = rows // BLK
    scale = math.log2(math.e) * HD ** -0.5

    loads = [
        pltpu.make_async_copy(cond_hbm, xall.at[pl.ds(rows, crows)], load_sem.at[0]),
        pltpu.make_async_copy(x_hbm, xall.at[pl.ds(0, rows)], load_sem.at[1]),
        pltpu.make_async_copy(wk_hbm, wk, load_sem.at[2]),
        pltpu.make_async_copy(wv_hbm, wv, load_sem.at[3]),
        pltpu.make_async_copy(lists_hbm, lsend, load_sem.at[4]),
        pltpu.make_async_copy(wq_hbm, wq, load_sem.at[5]),
        pltpu.make_async_copy(wo_hbm, wo, load_sem.at[6]),
    ]
    for load in loads:
        load.start()

    barrier = pltpu.get_barrier_semaphore()

    def greet_view(i, c):
        pl.semaphore_signal(
            barrier, inc=1, device_id=(lax.rem(view + i, nview), tok), device_id_type=MESH
        )
        return c

    def greet_tok(i, c):
        pl.semaphore_signal(
            barrier, inc=1, device_id=(view, lax.rem(tok + i, ntok)), device_id_type=MESH
        )
        return c

    lax.fori_loop(1, nview, greet_view, 0)
    lax.fori_loop(1, ntok, greet_tok, 0)

    low = lax.broadcasted_iota(jnp.int32, (1, 2 * HD), 1) < HD

    for load in loads[:5]:
        load.wait()

    def project_kv(j, c):
        columns = pl.ds(pl.multiple_of(j * 256, 256), 256)
        keys = dot(xall[...], wk[:, columns])
        values = dot(xall[...], wv[:, columns])
        for p in range(2):
            k = keys[:, p * 128 : (p + 1) * 128]
            v = pltpu.roll(values[:, p * 128 : (p + 1) * 128], HD, 1)
            even = jnp.where(low, k, v).astype(jnp.bfloat16)
            odd = jnp.where(low, v, k).astype(jnp.bfloat16)
            kvsend[4 * j + 2 * p] = even[:rows].reshape(nblk, BLK, 2 * HD)
            kvsend[4 * j + 2 * p + 1] = odd[:rows].reshape(nblk, BLK, 2 * HD)
            csend[4 * j + 2 * p] = even[rows:]
            csend[4 * j + 2 * p + 1] = odd[rows:]
        return c

    lax.fori_loop(0, width // 256, project_kv, 0)

    pl.semaphore_wait(barrier, nview + ntok - 2)

    def view_copy(i, name):
        to = lax.rem(view + i, nview)
        target = (to, tok)

        def remote(src, dst, send, recv):
            return pltpu.make_async_remote_copy(
                src_ref=src, dst_ref=dst, send_sem=send.at[i], recv_sem=recv.at[i],
                device_id=target, device_id_type=MESH,
            )

        if name == "c":
            return remote(csend.at[to], condkv.at[tok, view], c_ss, c_rs)
        if name == "l":
            return remote(lsend, lists_v.at[view], l_ss, l_rs)
        if name == "q":
            return remote(qsend.at[to], qrecv.at[view], q_ss, q_rs)
        own = pool.at[pl.ds((nview + view) * nblk, nblk)]
        return remote(kvsend.at[to], own, kv_ss, kv_rs)

    def start(*names):
        def body(i, c):
            for name in names:
                view_copy(i, name).start()
            return c

        lax.fori_loop(1, nview, body, 0)

    start("c", "l")
    condkv[tok, view] = csend[view]
    lists_v[view] = lsend[...]

    loads[5].wait()

    def project_q(j, c):
        columns = pl.ds(pl.multiple_of(j * 256, 256), 256)
        query = dot(xall[pl.ds(0, rows), :], wq[:, columns])
        for p in range(2):
            first = query[:half, p * 128 : (p + 1) * 128]
            second = pltpu.roll(query[half:, p * 128 : (p + 1) * 128], HD, 1)
            qsend[4 * j + 2 * p] = jnp.where(low, first, second).astype(jnp.bfloat16)
            qsend[4 * j + 2 * p + 1] = jnp.where(low, second, first).astype(jnp.bfloat16)
        return c

    lax.fori_loop(0, width // 256, project_q, 0)
    start("q")
    start("kv")
    qrecv[view] = qsend[view]
    pool[pl.ds((nview + view) * nblk, nblk)] = kvsend[view]

    def wait_view(name, start_i=1):
        def body(i, c):
            view_copy(i, name).wait_recv()
            return c

        lax.fori_loop(start_i, nview, body, 0)

    wait_view("c")

    def tok_copy(i):
        return pltpu.make_async_remote_copy(
            src_ref=condkv.at[tok], dst_ref=condkv.at[tok],
            send_sem=g_ss.at[i], recv_sem=g_rs.at[i],
            device_id=(view, lax.rem(tok + i, ntok)), device_id_type=MESH,
        )

    def start_tok(i, c):
        tok_copy(i).start()
        return c

    def wait_tok(i, c):
        tok_copy(i).wait_recv()
        return c

    lax.fori_loop(1, ntok, start_tok, 0)
    lax.fori_loop(1, ntok, wait_tok, 0)

    parity = lax.rem(view, 2)
    lane = lax.broadcasted_iota(jnp.int32, (1, 2 * HD), 1)
    khalf = (lane // HD) == parity
    kf = jnp.where(khalf, 1.0, 0.0)
    krow = kf.astype(jnp.bfloat16)
    vrow = (1.0 - kf).astype(jnp.bfloat16)
    count = ntok * nview * crows

    pool[3 * nview * nblk] = condkv[0, pl.ds(0, BLK // crows)].reshape(BLK, 2 * HD)
    vcond[...] = condkv[...].reshape(count, 2 * HD) * vrow + krow

    def forward(i, direction):
        at = pl.ds((nview + lax.rem(view - i + nview, nview)) * nblk, nblk)
        to = pl.ds((2 * direction * nview + lax.rem(view - i + nview, nview)) * nblk, nblk)
        step = 1 if direction == 0 else ntok - 1
        return pltpu.make_async_remote_copy(
            src_ref=pool.at[at], dst_ref=pool.at[to],
            send_sem=f_ss.at[direction, i], recv_sem=f_rs.at[direction, i],
            device_id=(view, lax.rem(tok + step, ntok)), device_id_type=MESH,
        )

    forward(0, 0).start()
    forward(0, 1).start()

    def pass_on(i):
        view_copy(i, "kv").wait_recv()
        forward(i, 0).start()
        forward(i, 1).start()

    def cond_step(i, c):
        @pl.when(i > 0)
        def _():
            view_copy(i, "q").wait_recv()

        owner = lax.rem(view - i + nview, nview)
        packed = qrecv[owner].astype(jnp.float32)
        qpad[i, pl.ds(0, half)] = jnp.where(khalf, packed, 0.0).astype(jnp.bfloat16)
        qpad[i, pl.ds(half, half)] = jnp.where(khalf, pltpu.roll(packed, HD, 1), 0.0).astype(
            jnp.bfloat16
        )
        ck = condkv[...].reshape(count, 2 * HD)
        for part in range(2):
            at = pl.ds(part * half, half)
            scores = dot_t(qpad[i, at], ck)
            peak = jnp.max(scores, axis=1, keepdims=True)
            weights = jnp.exp2((scores - peak) * scale).astype(jnp.bfloat16)
            oacc[i, at] = dot(weights, vcond[...])
            mrow[i, at] = jnp.broadcast_to(peak, (half, 2 * HD))

        @pl.when(i > LAG)
        def _():
            pass_on(i - LAG)

        return c

    lax.fori_loop(0, nview, cond_step, 0)

    def rest(i, c):
        pass_on(i)
        return c

    lax.fori_loop(nview - LAG, nview, rest, 0)
    wait_view("l")
    to_smem = pltpu.make_async_copy(lists_v, lists_s, smem_sem)
    to_smem.start()
    to_smem.wait()

    def wait_forward(i, c):
        forward(i, 0).wait_recv()
        forward(i, 1).wait_recv()
        return c

    lax.fori_loop(0, nview, wait_forward, 0)

    def o_copy(i):
        return pltpu.make_async_remote_copy(
            src_ref=osend.at[i], dst_ref=orecv.at[view],
            send_sem=o_ss.at[i], recv_sem=o_rs.at[i],
            device_id=(lax.rem(view - i + nview, nview), tok), device_id_type=MESH,
        )

    def epi_step(i, c):
        owner = lax.rem(view - i + nview, nview)
        parts = []
        for b in range(nblk):
            at = pl.ds(b * BLK, BLK)
            kvs, vvs = [], []
            for s in range(most):
                entry = lists_s[owner, 0, b * most + s]
                used = jnp.where(entry < 3 * nview * nblk, 1.0, 0.0)
                block = pool[entry]
                kvs.append(block)
                vvs.append(
                    block * ((1.0 - kf) * used).astype(jnp.bfloat16)
                    + (kf * used).astype(jnp.bfloat16)
                )
            scores = dot_t(qpad[i, at], jnp.concatenate(kvs, axis=0))
            before = mrow[i, at]
            peak = jnp.maximum(before[:, :1], jnp.max(scores, axis=1, keepdims=True))
            weights = jnp.exp2((scores - peak) * scale).astype(jnp.bfloat16)
            total = oacc[i, at] * jnp.exp2((before - peak) * scale) + dot(
                weights, jnp.concatenate(vvs, axis=0)
            )
            parts.append(total / pltpu.roll(total, HD, 1))
        first = jnp.concatenate(parts[: nblk // 2], axis=0)
        second = pltpu.roll(jnp.concatenate(parts[nblk // 2 :], axis=0), HD, 1)
        osend[i] = jnp.where(khalf, second, first).astype(jnp.bfloat16)

        @pl.when(i > 0)
        def _():
            o_copy(i).start()

        @pl.when(i == 0)
        def _():
            orecv[view] = osend[i]

        return c

    lax.fori_loop(0, nview, epi_step, 0)

    loads[6].wait()

    def wait_o(i, c):
        o_copy(i).wait_recv()
        return c

    lax.fori_loop(1, nview, wait_o, 0)

    for j in range(nview // 2):
        even = orecv[2 * j].astype(jnp.float32)
        odd = orecv[2 * j + 1].astype(jnp.float32)
        at = pl.ds(j * 128, 128)
        att[pl.ds(0, half), at] = pltpu.roll(jnp.where(low, odd, even), HD, 1).astype(jnp.bfloat16)
        att[pl.ds(half, half), at] = jnp.where(low, even, odd).astype(jnp.bfloat16)

    def project_out(j, c):
        columns = pl.ds(pl.multiple_of(j * 256, 256), 256)
        outv[:, columns] = dot(att[...], wo[:, columns]).astype(jnp.bfloat16)
        return c

    lax.fori_loop(0, width // 256, project_out, 0)
    store = pltpu.make_async_copy(outv, out_hbm, out_sem)
    store.start()

    def wait_sends(i, c):
        for name in ("c", "l", "q", "kv"):
            view_copy(i, name).wait_send()
        o_copy(i).wait_send()
        return c

    def wait_tok_sends(i, c):
        tok_copy(i).wait_send()
        return c

    def wait_forward_sends(i, c):
        forward(i, 0).wait_send()
        forward(i, 1).wait_send()
        return c

    lax.fori_loop(1, nview, wait_sends, 0)
    lax.fori_loop(1, ntok, wait_tok_sends, 0)
    lax.fori_loop(0, nview, wait_forward_sends, 0)
    store.wait()


def local(x_target, cond_x, w_query, w_key, w_value, w_out, epi_lists):
    nview = lax.axis_size("view")
    ntok = lax.axis_size("tok")
    rows, width = x_target.shape[1:]
    crows = cond_x.shape[0]
    most = epi_lists.shape[2]
    nblk = rows // BLK
    band = lax.axis_index("tok")
    entry_view = epi_lists[0, :, :, 0].reshape(-1)
    entry_block = epi_lists[0, :, :, 1].reshape(-1) - (band - 1) * nblk
    place = ((entry_block // nblk) * nview + entry_view) * nblk + entry_block % nblk
    place = jnp.where(entry_view >= 0, place, 3 * nview * nblk)
    lists = jnp.zeros((8, 128), jnp.int32).at[0, : nblk * most].set(place)
    bf, f32 = jnp.bfloat16, jnp.float32
    half = rows // 2
    dma = pltpu.SemaphoreType.DMA
    scratch = [
        pltpu.VMEM((rows + crows, width), bf),
        pltpu.VMEM((width, width), bf),
        pltpu.VMEM((width, width), bf),
        pltpu.VMEM((width, width), bf),
        pltpu.VMEM((width, width), bf),
        pltpu.VMEM((nview, half, 128), bf),
        pltpu.VMEM((nview, nblk, BLK, 128), bf),
        pltpu.VMEM((nview, crows, 128), bf),
        pltpu.VMEM((8, 128), jnp.int32),
        pltpu.VMEM((nview, half, 128), bf),
        pltpu.VMEM((3 * nview * nblk + 1, BLK, 128), bf),
        pltpu.VMEM((ntok, nview, crows, 128), bf),
        pltpu.VMEM((nview, 8, 128), jnp.int32),
        pltpu.SMEM((nview, 8, 128), jnp.int32),
        pltpu.VMEM((ntok * nview * crows, 128), bf),
        pltpu.VMEM((nview, rows, 128), bf),
        pltpu.VMEM((nview, rows, 128), f32),
        pltpu.VMEM((nview, rows, 128), f32),
        pltpu.VMEM((nview, half, 128), bf),
        pltpu.VMEM((nview, half, 128), bf),
        pltpu.VMEM((rows, width), bf),
        pltpu.VMEM((rows, width), bf),
        dma((7,)),
        *[dma((nview,)) for _ in range(8)],
        dma((ntok,)), dma((ntok,)),
        dma((2, nview)), dma((2, nview)),
        dma((nview,)), dma((nview,)),
        dma, dma,
    ]
    mixed = pl.pallas_call(
        functools.partial(kernel, nview, ntok, rows, crows, most),
        out_shape=jax.ShapeDtypeStruct((rows, width), bf),
        in_specs=[pl.BlockSpec(memory_space=pl.ANY)] * 7,
        out_specs=pl.BlockSpec(memory_space=pl.ANY),
        scratch_shapes=scratch,
        compiler_params=pltpu.CompilerParams(
            collective_id=0, has_side_effects=True, vmem_limit_bytes=60 * 1024 * 1024
        ),
    )(x_target[0], cond_x, w_query, w_key, w_value, w_out, lists)
    return mixed[None]


def solution(mesh):
    placed = (
        P("view", "tok", None),
        P(("view", "tok"), None),
        P(),
        P(),
        P(),
        P(),
        P("view", "tok", None, None),
    )
    return jax.shard_map(
        local, mesh=mesh, in_specs=placed, out_specs=P("view", "tok", None), check_vma=False
    )
```

```python
import functools
import math

import jax
import jax.numpy as jnp
from jax import lax
from jax.experimental import pallas as pl
from jax.experimental.pallas import tpu as pltpu
from jax.sharding import PartitionSpec as P

HD = 64
BLK = 128
MESH = pl.DeviceIdType.MESH
LAG = 2
CHUNKS = 1


def dot(a, b):
    return jnp.dot(a, b, preferred_element_type=jnp.float32)


def dot_t(a, b):
    return lax.dot_general(a, b, (((1,), (1,)), ((), ())), preferred_element_type=jnp.float32)


def kernel(
    nview, ntok, side, rows, crows, most,
    x_hbm, cond_hbm, wq_hbm, wk_hbm, wv_hbm, lists_hbm,
    out_hbm,
    xall, wq, wk, wv,
    qsend, kvsend, csend, lsend,
    qrecv, pool, condkv, lists_v, lists_s,
    vcond, qpad, oacc, mrow, osend, orecv, att,
    load_sem, q_ss, q_rs, kv_ss, kv_rs, c_ss, c_rs, l_ss, l_rs, g_ss, g_rs, f_ss, f_rs, o_ss, o_rs, smem_sem, out_sem,
):
    view = lax.axis_index("view")
    tok = lax.axis_index("tok")
    width = nview * HD
    half = rows // 2
    nblk = rows // BLK
    scale = math.log2(math.e) * HD ** -0.5

    loads = [
        pltpu.make_async_copy(cond_hbm, xall.at[pl.ds(rows, crows)], load_sem.at[0]),
        pltpu.make_async_copy(x_hbm, xall.at[pl.ds(0, rows)], load_sem.at[1]),
        pltpu.make_async_copy(wk_hbm, wk, load_sem.at[2]),
        pltpu.make_async_copy(wv_hbm, wv, load_sem.at[3]),
        pltpu.make_async_copy(lists_hbm, lsend, load_sem.at[4]),
        pltpu.make_async_copy(wq_hbm, wq, load_sem.at[5]),
    ]
    for load in loads:
        load.start()

    barrier = pltpu.get_barrier_semaphore()

    def peer(i, sign):
        dx, dy = lax.rem(i, side), lax.rem(i + i // side, side)
        x = lax.rem(view // side + sign * dx + side, side)
        y = lax.rem(lax.rem(view, side) + sign * dy + side, side)
        return x * side + y

    def greet_view(i, c):
        pl.semaphore_signal(barrier, inc=1, device_id=(peer(i, 1), tok), device_id_type=MESH)
        return c

    def greet_tok(i, c):
        pl.semaphore_signal(
            barrier, inc=1, device_id=(view, lax.rem(tok + i, ntok)), device_id_type=MESH
        )
        return c

    lax.fori_loop(1, nview, greet_view, 0)
    lax.fori_loop(1, ntok, greet_tok, 0)

    low = lax.broadcasted_iota(jnp.int32, (1, 2 * HD), 1) < HD

    for load in loads[:5]:
        load.wait()

    def project_kv(j, c):
        columns = pl.ds(pl.multiple_of(j * 256, 256), 256)
        keys = dot(xall[...], wk[:, columns])
        values = dot(xall[...], wv[:, columns])
        for p in range(2):
            k = keys[:, p * 128 : (p + 1) * 128]
            v = pltpu.roll(values[:, p * 128 : (p + 1) * 128], HD, 1)
            even = jnp.where(low, k, v).astype(jnp.bfloat16)
            odd = jnp.where(low, v, k).astype(jnp.bfloat16)
            kvsend[4 * j + 2 * p] = even[:rows].reshape(nblk, BLK, 2 * HD)
            kvsend[4 * j + 2 * p + 1] = odd[:rows].reshape(nblk, BLK, 2 * HD)
            csend[4 * j + 2 * p] = even[rows:]
            csend[4 * j + 2 * p + 1] = odd[rows:]
        return c

    lax.fori_loop(0, width // 256, project_kv, 0)

    pl.semaphore_wait(barrier, nview + ntok - 2)

    piece = nblk // CHUNKS

    def view_copy(i, name, part=0):
        to = peer(i, 1)
        target = (to, tok)

        def remote(src, dst, send, recv):
            at = part * nview + i
            return pltpu.make_async_remote_copy(
                src_ref=src, dst_ref=dst, send_sem=send.at[at], recv_sem=recv.at[at],
                device_id=target, device_id_type=MESH,
            )

        if name == "c":
            return remote(csend.at[to], condkv.at[tok, view], c_ss, c_rs)
        if name == "l":
            return remote(lsend, lists_v.at[view], l_ss, l_rs)
        if name == "q":
            return remote(qsend.at[to], qrecv.at[view], q_ss, q_rs)
        own = pool.at[pl.ds((nview + view) * nblk + part * piece, piece)]
        return remote(kvsend.at[to, pl.ds(part * piece, piece)], own, kv_ss, kv_rs)

    def start(*names, part=0):
        def body(i, c):
            for name in names:
                view_copy(i, name, part).start()
            return c

        lax.fori_loop(1, nview, body, 0)

    start("c", "l")
    condkv[tok, view] = csend[view]
    lists_v[view] = lsend[...]

    loads[5].wait()

    def project_q(j, c):
        columns = pl.ds(pl.multiple_of(j * 256, 256), 256)
        query = dot(xall[pl.ds(0, rows), :], wq[:, columns])
        for p in range(2):
            first = query[:half, p * 128 : (p + 1) * 128]
            second = pltpu.roll(query[half:, p * 128 : (p + 1) * 128], HD, 1)
            qsend[4 * j + 2 * p] = jnp.where(low, first, second).astype(jnp.bfloat16)
            qsend[4 * j + 2 * p + 1] = jnp.where(low, second, first).astype(jnp.bfloat16)
        return c

    lax.fori_loop(0, width // 256, project_q, 0)
    start("q")
    for part in range(CHUNKS):
        start("kv", part=part)
    qrecv[view] = qsend[view]
    pool[pl.ds((nview + view) * nblk, nblk)] = kvsend[view]

    def wait_view(name, start_i=1):
        def body(i, c):
            view_copy(i, name).wait_recv()
            return c

        lax.fori_loop(start_i, nview, body, 0)

    wait_view("c")

    def tok_copy(i):
        return pltpu.make_async_remote_copy(
            src_ref=condkv.at[tok], dst_ref=condkv.at[tok],
            send_sem=g_ss.at[i], recv_sem=g_rs.at[i],
            device_id=(view, lax.rem(tok + i, ntok)), device_id_type=MESH,
        )

    def start_tok(i, c):
        tok_copy(i).start()
        return c

    def wait_tok(i, c):
        tok_copy(i).wait_recv()
        return c

    lax.fori_loop(1, ntok, start_tok, 0)
    lax.fori_loop(1, ntok, wait_tok, 0)

    parity = lax.rem(view, 2)
    lane = lax.broadcasted_iota(jnp.int32, (1, 2 * HD), 1)
    khalf = (lane // HD) == parity
    kf = jnp.where(khalf, 1.0, 0.0)
    krow = kf.astype(jnp.bfloat16)
    vrow = (1.0 - kf).astype(jnp.bfloat16)
    count = ntok * nview * crows

    pool[3 * nview * nblk] = condkv[0, pl.ds(0, BLK // crows)].reshape(BLK, 2 * HD)
    vcond[...] = condkv[...].reshape(count, 2 * HD) * vrow + krow

    def forward(i, part, direction):
        owner = peer(i, -1) * nblk + part * piece
        at = pl.ds(nview * nblk + owner, piece)
        to = pl.ds(2 * direction * nview * nblk + owner, piece)
        step = 1 if direction == 0 else ntok - 1
        sem = part * nview + i
        return pltpu.make_async_remote_copy(
            src_ref=pool.at[at], dst_ref=pool.at[to],
            send_sem=f_ss.at[direction, sem], recv_sem=f_rs.at[direction, sem],
            device_id=(view, lax.rem(tok + step, ntok)), device_id_type=MESH,
        )

    for part in range(CHUNKS):
        forward(0, part, 0).start()
        forward(0, part, 1).start()

    units = CHUNKS * (nview - 1)

    def pass_on(u):
        part, i = u // (nview - 1), 1 + lax.rem(u, nview - 1)
        view_copy(i, "kv", part).wait_recv()
        forward(i, part, 0).start()
        forward(i, part, 1).start()

    def cond_step(i, c):
        @pl.when(i > 0)
        def _():
            view_copy(i, "q").wait_recv()

        packed = qrecv[peer(i, -1)].astype(jnp.float32)
        qpad[i, pl.ds(0, half)] = jnp.where(khalf, packed, 0.0).astype(jnp.bfloat16)
        qpad[i, pl.ds(half, half)] = jnp.where(khalf, pltpu.roll(packed, HD, 1), 0.0).astype(
            jnp.bfloat16
        )
        ck = condkv[...].reshape(count, 2 * HD)
        scores = [dot_t(qpad[i, pl.ds(part * half, half)], ck) for part in range(2)]
        for part in range(2):
            at = pl.ds(part * half, half)
            peak = jnp.max(scores[part], axis=1, keepdims=True)
            weights = jnp.exp2((scores[part] - peak) * scale).astype(jnp.bfloat16)
            oacc[i, at] = dot(weights, vcond[...])
            mrow[i, at] = jnp.broadcast_to(peak, (half, 2 * HD))

        @pl.when(i >= LAG)
        def _():
            pass_on(CHUNKS * (i - LAG))

        return c

    lax.fori_loop(0, nview, cond_step, 0)

    def rest(i, c):
        pass_on(i)
        return c

    lax.fori_loop(CHUNKS * (nview - LAG), units, rest, 0)
    wait_view("l")
    to_smem = pltpu.make_async_copy(lists_v, lists_s, smem_sem)
    to_smem.start()
    to_smem.wait()

    def wait_forward(i, c):
        for part in range(CHUNKS):
            forward(i, part, 0).wait_recv()
            forward(i, part, 1).wait_recv()
        return c

    lax.fori_loop(0, nview, wait_forward, 0)

    def o_copy(i):
        return pltpu.make_async_remote_copy(
            src_ref=osend.at[i], dst_ref=orecv.at[view],
            send_sem=o_ss.at[i], recv_sem=o_rs.at[i],
            device_id=(peer(i, -1), tok), device_id_type=MESH,
        )

    def epi_step(j, c):
        i = lax.rem(j + 1, nview)
        owner = peer(i, -1)
        scores, values, parts = [], [], []
        for b in range(nblk):
            kvs, vvs = [], []
            for s in range(most):
                entry = lists_s[owner, b, s]
                used = jnp.where(entry < 3 * nview * nblk, 1.0, 0.0)
                block = pool[entry]
                kvs.append(block)
                vvs.append(
                    block * ((1.0 - kf) * used).astype(jnp.bfloat16)
                    + (kf * used).astype(jnp.bfloat16)
                )
            scores.append(dot_t(qpad[i, pl.ds(b * BLK, BLK)], jnp.concatenate(kvs, axis=0)))
            values.append(jnp.concatenate(vvs, axis=0))
        for b in range(nblk):
            at = pl.ds(b * BLK, BLK)
            before = mrow[i, at]
            peak = jnp.maximum(before[:, :1], jnp.max(scores[b], axis=1, keepdims=True))
            weights = jnp.exp2((scores[b] - peak) * scale).astype(jnp.bfloat16)
            total = oacc[i, at] * jnp.exp2((before - peak) * scale) + dot(weights, values[b])
            parts.append(total / pltpu.roll(total, HD, 1))
        first = jnp.concatenate(parts[: nblk // 2], axis=0)
        second = pltpu.roll(jnp.concatenate(parts[nblk // 2 :], axis=0), HD, 1)
        osend[i] = jnp.where(khalf, second, first).astype(jnp.bfloat16)

        @pl.when(i > 0)
        def _():
            o_copy(i).start()

        @pl.when(i == 0)
        def _():
            orecv[view] = osend[i]

        return c

    lax.fori_loop(0, nview, epi_step, 0)

    def wait_o(i, c):
        o_copy(i).wait_recv()
        return c

    lax.fori_loop(1, nview, wait_o, 0)

    for j in range(nview // 2):
        even = orecv[2 * j].astype(jnp.float32)
        odd = orecv[2 * j + 1].astype(jnp.float32)
        at = pl.ds(j * 128, 128)
        att[pl.ds(0, half), at] = pltpu.roll(jnp.where(low, odd, even), HD, 1).astype(jnp.bfloat16)
        att[pl.ds(half, half), at] = jnp.where(low, even, odd).astype(jnp.bfloat16)

    store = pltpu.make_async_copy(att, out_hbm, out_sem)
    store.start()

    def wait_sends(i, c):
        for name in ("c", "l", "q"):
            view_copy(i, name).wait_send()
        for part in range(CHUNKS):
            view_copy(i, "kv", part).wait_send()
        o_copy(i).wait_send()
        return c

    def wait_tok_sends(i, c):
        tok_copy(i).wait_send()
        return c

    def wait_forward_sends(i, c):
        for part in range(CHUNKS):
            forward(i, part, 0).wait_send()
            forward(i, part, 1).wait_send()
        return c

    lax.fori_loop(1, nview, wait_sends, 0)
    lax.fori_loop(1, ntok, wait_tok_sends, 0)
    lax.fori_loop(0, nview, wait_forward_sends, 0)
    store.wait()


def local(x_target, cond_x, w_query, w_key, w_value, w_out, epi_lists):
    nview = lax.axis_size("view")
    ntok = lax.axis_size("tok")
    rows, width = x_target.shape[1:]
    crows = cond_x.shape[0]
    most = epi_lists.shape[2]
    nblk = rows // BLK
    band = lax.axis_index("tok")
    entry_view = epi_lists[0, :, :, 0]
    entry_block = epi_lists[0, :, :, 1] - (band - 1) * nblk
    place = ((entry_block // nblk) * nview + entry_view) * nblk + entry_block % nblk
    place = jnp.where(entry_view >= 0, place, 3 * nview * nblk)
    lists = jnp.pad(place, ((0, 8 - nblk), (0, 128 - most)))
    bf, f32 = jnp.bfloat16, jnp.float32
    half = rows // 2
    dma = pltpu.SemaphoreType.DMA
    scratch = [
        pltpu.VMEM((rows + crows, width), bf),
        pltpu.VMEM((width, width), bf),
        pltpu.VMEM((width, width), bf),
        pltpu.VMEM((width, width), bf),
        pltpu.VMEM((nview, half, 128), bf),
        pltpu.VMEM((nview, nblk, BLK, 128), bf),
        pltpu.VMEM((nview, crows, 128), bf),
        pltpu.VMEM((8, 128), jnp.int32),
        pltpu.VMEM((nview, half, 128), bf),
        pltpu.VMEM((3 * nview * nblk + 1, BLK, 128), bf),
        pltpu.VMEM((ntok, nview, crows, 128), bf),
        pltpu.VMEM((nview, 8, 128), jnp.int32),
        pltpu.SMEM((nview, 8, 128), jnp.int32),
        pltpu.VMEM((ntok * nview * crows, 128), bf),
        pltpu.VMEM((nview, rows, 128), bf),
        pltpu.VMEM((nview, rows, 128), f32),
        pltpu.VMEM((nview, rows, 128), f32),
        pltpu.VMEM((nview, half, 128), bf),
        pltpu.VMEM((nview, half, 128), bf),
        pltpu.VMEM((rows, width), bf),
        dma((6,)),
        dma((nview,)), dma((nview,)),
        dma((CHUNKS * nview,)), dma((CHUNKS * nview,)),
        *[dma((nview,)) for _ in range(4)],
        dma((ntok,)), dma((ntok,)),
        dma((2, CHUNKS * nview)), dma((2, CHUNKS * nview)),
        dma((nview,)), dma((nview,)),
        dma, dma,
    ]
    attended = pl.pallas_call(
        functools.partial(kernel, nview, ntok, math.isqrt(nview), rows, crows, most),
        out_shape=jax.ShapeDtypeStruct((rows, width), bf),
        in_specs=[pl.BlockSpec(memory_space=pl.ANY)] * 6,
        out_specs=pl.BlockSpec(memory_space=pl.ANY),
        scratch_shapes=scratch,
        compiler_params=pltpu.CompilerParams(
            collective_id=0, has_side_effects=True, vmem_limit_bytes=60 * 1024 * 1024
        ),
    )(x_target[0], cond_x, w_query, w_key, w_value, lists)
    return dot(attended, w_out).astype(bf)[None]


def solution(mesh):
    placed = (
        P("view", "tok", None),
        P(("view", "tok"), None),
        P(),
        P(),
        P(),
        P(),
        P("view", "tok", None, None),
    )
    return jax.shard_map(
        local, mesh=mesh, in_specs=placed, out_specs=P("view", "tok", None), check_vma=False
    )
```

```python
import functools
import math

import jax
import jax.numpy as jnp
from jax import lax
from jax.experimental import pallas as pl
from jax.experimental.pallas import tpu as pltpu
from jax.sharding import PartitionSpec as P

HD = 64
BLK = 128
MESH = pl.DeviceIdType.MESH
LAG = 2
FIRST = 7
VPS = 2


def dot(a, b):
    return jnp.dot(a, b, preferred_element_type=jnp.float32)


def dot_t(a, b):
    return lax.dot_general(a, b, (((1,), (1,)), ((), ())), preferred_element_type=jnp.float32)


def kernel(
    nview, ntok, side, rows, crows, most,
    x_hbm, cond_hbm, wq_hbm, wk_hbm, wv_hbm, lists_hbm,
    out_hbm,
    xall, wq, wk, wv,
    qsend, ksend, vsend, csend, lsend,
    qrecv, kpool, vpool, condkv, lists_v, lists_s,
    vcond, qstk, acc_t, peak_t, osend, orecv, att,
    load_sem, q_ss, q_rs, kv_ss, kv_rs, c_ss, c_rs, l_ss, l_rs, g_ss, g_rs, f_ss, f_rs, o_ss, o_rs, smem_sem, out_sem,
):
    view = lax.axis_index("view")
    tok = lax.axis_index("tok")
    width = nview * HD
    half = rows // 2
    nblk = rows // BLK
    scale = math.log2(math.e) * HD ** -0.5

    loads = [
        pltpu.make_async_copy(x_hbm, xall.at[pl.ds(0, rows)], load_sem.at[0]),
        pltpu.make_async_copy(wq_hbm, wq, load_sem.at[1]),
        pltpu.make_async_copy(cond_hbm, xall.at[pl.ds(rows, crows)], load_sem.at[2]),
        pltpu.make_async_copy(wk_hbm, wk, load_sem.at[3]),
        pltpu.make_async_copy(wv_hbm, wv, load_sem.at[4]),
        pltpu.make_async_copy(lists_hbm, lsend, load_sem.at[5]),
    ]
    for load in loads:
        load.start()

    barrier = pltpu.get_barrier_semaphore()

    def peer(i, sign):
        dx, dy = lax.rem(i, side), lax.rem(i + i // side, side)
        x = lax.rem(view // side + sign * dx + side, side)
        y = lax.rem(lax.rem(view, side) + sign * dy + side, side)
        return x * side + y

    def greet_view(i, c):
        pl.semaphore_signal(barrier, inc=1, device_id=(peer(i, 1), tok), device_id_type=MESH)
        return c

    def greet_tok(i, c):
        pl.semaphore_signal(
            barrier, inc=1, device_id=(view, lax.rem(tok + i, ntok)), device_id_type=MESH
        )
        return c

    lax.fori_loop(1, nview, greet_view, 0)
    lax.fori_loop(1, ntok, greet_tok, 0)

    low = lax.broadcasted_iota(jnp.int32, (1, 2 * HD), 1) < HD

    def split(x, count):
        x = x.reshape(count, 2, -1, 2 * HD)
        first = x[:, 0].reshape(-1, 2 * HD)
        second = pltpu.roll(x[:, 1].reshape(-1, 2 * HD), HD, 1)
        even = jnp.where(low, first, second).astype(jnp.bfloat16)
        odd = jnp.where(low, second, first).astype(jnp.bfloat16)
        return even, odd

    def project_q(j, c):
        columns = pl.ds(pl.multiple_of(j * 256, 256), 256)
        query = dot(xall[pl.ds(0, rows), :], wq[:, columns])
        for p in range(2):
            even, odd = split(query[:, p * 128 : (p + 1) * 128], 1)
            qsend[4 * j + 2 * p] = even
            qsend[4 * j + 2 * p + 1] = odd
        return c

    loads[0].wait()
    loads[1].wait()
    lax.fori_loop(0, width // 256, project_q, 0)

    pl.semaphore_wait(barrier, nview + ntok - 2)

    def view_copy(i, name):
        to = peer(i, 1)
        target = (to, tok)

        def remote(src, dst, send, recv, at):
            return pltpu.make_async_remote_copy(
                src_ref=src, dst_ref=dst, send_sem=send.at[at], recv_sem=recv.at[at],
                device_id=target, device_id_type=MESH,
            )

        own = pl.ds((nview + view) * nblk, nblk)
        if name == "c":
            return remote(csend.at[to], condkv.at[tok, view], c_ss, c_rs, i)
        if name == "l":
            return remote(lsend, lists_v.at[view], l_ss, l_rs, i)
        if name == "q":
            return remote(qsend.at[to], qrecv.at[view], q_ss, q_rs, i)
        if name == "k":
            return remote(ksend.at[to], kpool.at[own], kv_ss, kv_rs, i)
        return remote(vsend.at[to], vpool.at[own], kv_ss, kv_rs, nview + i)

    def start(*names, lo=1, hi=nview):
        def body(i, c):
            for name in names:
                view_copy(i, name).start()
            return c

        lax.fori_loop(lo, hi, body, 0)

    start("q", hi=1 + FIRST)
    for load in loads[2:]:
        load.wait()

    def project_kv(j, c):
        columns = pl.ds(pl.multiple_of(j * 256, 256), 256)
        keys = dot(xall[...], wk[:, columns])
        values = dot(xall[...], wv[:, columns])
        for p in range(2):
            head = 4 * j + 2 * p
            k = keys[:, p * 128 : (p + 1) * 128]
            v = values[:, p * 128 : (p + 1) * 128]
            for send, x in ((ksend, k), (vsend, v)):
                even, odd = split(x[:rows], nblk)
                send[head] = even.reshape(nblk, BLK // 2, 2 * HD)
                send[head + 1] = odd.reshape(nblk, BLK // 2, 2 * HD)
            k, v = k[rows:], pltpu.roll(v[rows:], HD, 1)
            csend[head] = jnp.where(low, k, v).astype(jnp.bfloat16)
            csend[head + 1] = jnp.where(low, v, k).astype(jnp.bfloat16)
        return c

    lax.fori_loop(0, width // 256, project_kv, 0)
    start("c", "l")
    start("q", lo=1 + FIRST)
    start("k", "v")
    condkv[tok, view] = csend[view]
    lists_v[view] = lsend[...]
    qrecv[view] = qsend[view]
    kpool[pl.ds((nview + view) * nblk, nblk)] = ksend[view]
    vpool[pl.ds((nview + view) * nblk, nblk)] = vsend[view]

    def wait_view(name, start_i=1):
        def body(i, c):
            view_copy(i, name).wait_recv()
            return c

        lax.fori_loop(start_i, nview, body, 0)

    wait_view("c")

    def tok_copy(i):
        return pltpu.make_async_remote_copy(
            src_ref=condkv.at[tok], dst_ref=condkv.at[tok],
            send_sem=g_ss.at[i], recv_sem=g_rs.at[i],
            device_id=(view, lax.rem(tok + i, ntok)), device_id_type=MESH,
        )

    def start_tok(i, c):
        tok_copy(i).start()
        return c

    def wait_tok(i, c):
        tok_copy(i).wait_recv()
        return c

    lax.fori_loop(1, ntok, start_tok, 0)
    lax.fori_loop(1, ntok, wait_tok, 0)

    parity = lax.rem(view, 2)
    lane = lax.broadcasted_iota(jnp.int32, (1, 2 * HD), 1)
    khalf = (lane // HD) == parity
    kf = jnp.where(khalf, 1.0, 0.0)
    krow = kf.astype(jnp.bfloat16)
    vrow = (1.0 - kf).astype(jnp.bfloat16)
    count = ntok * nview * crows

    spare = condkv[0, pl.ds(0, BLK // crows)].reshape(BLK, 2 * HD).astype(jnp.float32)
    kpool[3 * nview * nblk] = jnp.where(
        khalf, spare[: BLK // 2], pltpu.roll(spare[BLK // 2 :], HD, 1)
    ).astype(jnp.bfloat16)
    vpool[3 * nview * nblk] = jnp.zeros((BLK // 2, 2 * HD), jnp.bfloat16)
    vcond[...] = condkv[...].reshape(count, 2 * HD) * vrow + krow

    def forward(i, part, direction):
        owner = peer(i, -1) * nblk
        pool = (kpool, vpool)[part]
        step = 1 if direction == 0 else ntok - 1
        sem = part * nview + i
        return pltpu.make_async_remote_copy(
            src_ref=pool.at[pl.ds(nview * nblk + owner, nblk)],
            dst_ref=pool.at[pl.ds(2 * direction * nview * nblk + owner, nblk)],
            send_sem=f_ss.at[direction, sem], recv_sem=f_rs.at[direction, sem],
            device_id=(view, lax.rem(tok + step, ntok)), device_id_type=MESH,
        )

    for part in range(2):
        forward(0, part, 0).start()
        forward(0, part, 1).start()

    def pass_on(i):
        for part, name in enumerate("kv"):
            view_copy(i, name).wait_recv()
            forward(i, part, 0).start()
            forward(i, part, 1).start()

    def cond_step(i, c):
        @pl.when(i > 0)
        def _():
            view_copy(i, "q").wait_recv()

        packed = qrecv[peer(i, -1)].astype(jnp.float32)
        rolled = pltpu.roll(packed, HD, 1)
        first = [
            jnp.where(khalf, packed, 0.0).astype(jnp.bfloat16),
            jnp.where(khalf, rolled, 0.0).astype(jnp.bfloat16),
        ]
        other = [
            jnp.where(khalf, 0.0, rolled).astype(jnp.bfloat16),
            jnp.where(khalf, 0.0, packed).astype(jnp.bfloat16),
        ]
        ck = condkv[...].reshape(count, 2 * HD)
        scores = [dot_t(first[part], ck) for part in range(2)]
        for part in range(2):
            peak = jnp.max(scores[part], axis=1, keepdims=True)
            weights = jnp.exp2((scores[part] - peak) * scale).astype(jnp.bfloat16)
            total = dot(weights, vcond[...])
            peak = jnp.broadcast_to(peak, (half, 2 * HD))
            for b in range(nblk // 2):
                at = slice(b * BLK, (b + 1) * BLK)
                to = part * (nblk // 2) + b
                qstk[i, to, pl.ds(0, BLK)] = first[part][at]
                qstk[i, to, pl.ds(BLK, BLK)] = other[part][at]
                turned = total[at].T
                acc_t[i, to, pl.ds(0, HD)] = jnp.where(parity == 0, turned[HD:], turned[:HD])
                acc_t[i, to, pl.ds(HD, 8)] = jnp.where(
                    parity == 0, turned[:8], turned[HD : HD + 8]
                )
                peak_t[i, to] = peak[at].T[:8]

        @pl.when(i > LAG)
        def _():
            pass_on(i - LAG)

        return c

    lax.fori_loop(0, nview, cond_step, 0)

    def rest(i, c):
        pass_on(i)
        return c

    lax.fori_loop(nview - LAG, nview, rest, 0)
    wait_view("l")
    to_smem = pltpu.make_async_copy(lists_v, lists_s, smem_sem)
    to_smem.start()
    to_smem.wait()

    def wait_forward(i, c):
        for part in range(2):
            forward(i, part, 0).wait_recv()
            forward(i, part, 1).wait_recv()
        return c

    lax.fori_loop(0, nview, wait_forward, 0)

    def o_copy(i):
        return pltpu.make_async_remote_copy(
            src_ref=osend.at[i], dst_ref=orecv.at[view],
            send_sem=o_ss.at[i], recv_sem=o_rs.at[i],
            device_id=(peer(i, -1), tok), device_id_type=MESH,
        )

    half_lane = lane < HD

    def epi_step(j, c):
        steps = [lax.rem(VPS * j + a + 1, nview) for a in range(VPS)]
        work = [(i, peer(i, -1), b) for i in steps for b in range(nblk)]
        unused = 3 * nview * nblk
        scores, parts = [], []
        for i, owner, b in work:
            keys = jnp.concatenate([kpool[lists_s[owner, b, s]] for s in range(most)], axis=0)
            scores.append(dot_t(keys, qstk[i, b]))
        for (i, owner, b), score in zip(work, scores):
            before = peak_t[i, b][:1]
            peak = jnp.max(score, axis=0, keepdims=True)
            peak = jnp.maximum(jnp.maximum(peak[:, :BLK], peak[:, BLK:]), before)
            weights = jnp.exp2((score - jnp.concatenate([peak, peak], axis=1)) * scale)
            weights = weights.astype(jnp.bfloat16)
            fade = jnp.exp2((before - peak) * scale)
            entries = [lists_s[owner, b, s] for s in range(most)]
            used = [jnp.where(entry < unused, 1.0, 0.0) for entry in entries]
            values = jnp.concatenate([vpool[entry] for entry in entries], axis=0)
            sums = jnp.concatenate(
                [
                    jnp.broadcast_to(jnp.where(half_lane, used[s], used[s + 1]), (16, 2 * HD))
                    for s in range(0, most, 2)
                ],
                axis=1,
            ).astype(jnp.bfloat16)
            top = lax.dot_general(
                values, weights, (((0,), (0,)), ((), ())), preferred_element_type=jnp.float32
            )
            ones = dot(sums, weights)
            part = jnp.where(
                parity == 0,
                top[:HD, :BLK] + top[HD:, BLK:],
                top[HD:, :BLK] + top[:HD, BLK:],
            )
            total = ones[:1, :BLK] + ones[:1, BLK:] + acc_t[i, b, pl.ds(HD, 8)][:1] * fade
            parts.append((part + acc_t[i, b, pl.ds(0, HD)] * fade) / total)
        for a, i in enumerate(steps):
            mine = parts[a * nblk : (a + 1) * nblk]
            for b in range(nblk // 2):
                pair = jnp.concatenate([mine[b], mine[b + nblk // 2]], axis=0)
                osend[i, pl.ds(b * BLK, BLK)] = pair.T.astype(jnp.bfloat16)
            if a < VPS - 1:
                o_copy(i).start()
            else:

                @pl.when(i > 0)
                def _():
                    o_copy(i).start()

                @pl.when(i == 0)
                def _():
                    orecv[view] = osend[i]

        return c

    lax.fori_loop(0, nview // VPS, epi_step, 0)

    def wait_o(i, c):
        o_copy(i).wait_recv()
        return c

    lax.fori_loop(1, nview, wait_o, 0)

    for j in range(nview // 2):
        even = orecv[2 * j].astype(jnp.float32)
        odd = orecv[2 * j + 1].astype(jnp.float32)
        at = pl.ds(j * 128, 128)
        att[pl.ds(0, half), at] = jnp.where(low, even, pltpu.roll(odd, HD, 1)).astype(jnp.bfloat16)
        att[pl.ds(half, half), at] = jnp.where(low, pltpu.roll(even, HD, 1), odd).astype(
            jnp.bfloat16
        )

    store = pltpu.make_async_copy(att, out_hbm, out_sem)
    store.start()

    def wait_sends(i, c):
        for name in ("c", "l", "q", "k", "v"):
            view_copy(i, name).wait_send()
        o_copy(i).wait_send()
        return c

    def wait_tok_sends(i, c):
        tok_copy(i).wait_send()
        return c

    def wait_forward_sends(i, c):
        for part in range(2):
            forward(i, part, 0).wait_send()
            forward(i, part, 1).wait_send()
        return c

    lax.fori_loop(1, nview, wait_sends, 0)
    lax.fori_loop(1, ntok, wait_tok_sends, 0)
    lax.fori_loop(0, nview, wait_forward_sends, 0)
    store.wait()


def local(x_target, cond_x, w_query, w_key, w_value, w_out, epi_lists):
    nview = lax.axis_size("view")
    ntok = lax.axis_size("tok")
    rows, width = x_target.shape[1:]
    crows = cond_x.shape[0]
    most = epi_lists.shape[2]
    nblk = rows // BLK
    band = lax.axis_index("tok")
    entry_view = epi_lists[0, :, :, 0]
    entry_block = epi_lists[0, :, :, 1] - (band - 1) * nblk
    place = ((entry_block // nblk) * nview + entry_view) * nblk + entry_block % nblk
    place = jnp.where(entry_view >= 0, place, 3 * nview * nblk)
    lists = jnp.pad(place, ((0, 8 - nblk), (0, 128 - most)))
    bf, f32 = jnp.bfloat16, jnp.float32
    half = rows // 2
    dma = pltpu.SemaphoreType.DMA
    scratch = [
        pltpu.VMEM((rows + crows, width), bf),
        pltpu.VMEM((width, width), bf),
        pltpu.VMEM((width, width), bf),
        pltpu.VMEM((width, width), bf),
        pltpu.VMEM((nview, half, 128), bf),
        pltpu.VMEM((nview, nblk, BLK // 2, 128), bf),
        pltpu.VMEM((nview, nblk, BLK // 2, 128), bf),
        pltpu.VMEM((nview, crows, 128), bf),
        pltpu.VMEM((8, 128), jnp.int32),
        pltpu.VMEM((nview, half, 128), bf),
        pltpu.VMEM((3 * nview * nblk + 1, BLK // 2, 128), bf),
        pltpu.VMEM((3 * nview * nblk + 1, BLK // 2, 128), bf),
        pltpu.VMEM((ntok, nview, crows, 128), bf),
        pltpu.VMEM((nview, 8, 128), jnp.int32),
        pltpu.SMEM((nview, 8, 128), jnp.int32),
        pltpu.VMEM((ntok * nview * crows, 128), bf),
        pltpu.VMEM((nview, nblk, 2 * BLK, 128), bf),
        pltpu.VMEM((nview, nblk, HD + 8, BLK), f32),
        pltpu.VMEM((nview, nblk, 8, BLK), f32),
        pltpu.VMEM((nview, half, 128), bf),
        pltpu.VMEM((nview, half, 128), bf),
        pltpu.VMEM((rows, width), bf),
        dma((6,)),
        dma((nview,)), dma((nview,)),
        dma((2 * nview,)), dma((2 * nview,)),
        *[dma((nview,)) for _ in range(4)],
        dma((ntok,)), dma((ntok,)),
        dma((2, 2 * nview)), dma((2, 2 * nview)),
        dma((nview,)), dma((nview,)),
        dma, dma,
    ]
    attended = pl.pallas_call(
        functools.partial(kernel, nview, ntok, math.isqrt(nview), rows, crows, most),
        out_shape=jax.ShapeDtypeStruct((rows, width), bf),
        in_specs=[pl.BlockSpec(memory_space=pl.ANY)] * 6,
        out_specs=pl.BlockSpec(memory_space=pl.ANY),
        scratch_shapes=scratch,
        compiler_params=pltpu.CompilerParams(
            collective_id=0, has_side_effects=True, vmem_limit_bytes=60 * 1024 * 1024
        ),
    )(x_target[0], cond_x, w_query, w_key, w_value, lists)
    return dot(attended, w_out).astype(bf)[None]


def solution(mesh):
    placed = (
        P("view", "tok", None),
        P(("view", "tok"), None),
        P(),
        P(),
        P(),
        P(),
        P("view", "tok", None, None),
    )
    return jax.shard_map(
        local, mesh=mesh, in_specs=placed, out_specs=P("view", "tok", None), check_vma=False
    )
```

```python
import functools
import math

import jax
import jax.numpy as jnp
from jax import lax
from jax.experimental import pallas as pl
from jax.experimental.pallas import tpu as pltpu
from jax.sharding import PartitionSpec as P

HD = 64
BLK = 128
MESH = pl.DeviceIdType.MESH
LAG = 2
FIRST = 7
VPS = 2


def dot(a, b):
    return jnp.dot(a, b, preferred_element_type=jnp.float32)


def dot_t(a, b):
    return lax.dot_general(a, b, (((1,), (1,)), ((), ())), preferred_element_type=jnp.float32)


def kernel(
    nview, ntok, side, rows, crows, most,
    x_hbm, cond_hbm, wq_hbm, wk_hbm, wv_hbm, lists_hbm,
    out_hbm,
    xall, wq, wk, wv,
    qsend, ksend, vsend, csend, lraw, lsend,
    qrecv, kpool, vpool, condkv, lists_v, lists_s,
    vcond, qstk, acc_t, peak_t, osend, orecv, att,
    load_sem, q_ss, q_rs, kv_ss, kv_rs, c_ss, c_rs, l_ss, l_rs, g_ss, g_rs, f_ss, f_rs, o_ss, o_rs, smem_sem, out_sem,
):
    view = lax.axis_index("view")
    tok = lax.axis_index("tok")
    width = nview * HD
    half = rows // 2
    nblk = rows // BLK
    scale = math.log2(math.e) * HD ** -0.5

    loads = [
        pltpu.make_async_copy(x_hbm, xall.at[pl.ds(0, rows)], load_sem.at[0]),
        pltpu.make_async_copy(wq_hbm, wq, load_sem.at[1]),
        pltpu.make_async_copy(cond_hbm, xall.at[pl.ds(rows, crows)], load_sem.at[2]),
        pltpu.make_async_copy(wk_hbm, wk, load_sem.at[3]),
        pltpu.make_async_copy(wv_hbm, wv, load_sem.at[4]),
        pltpu.make_async_copy(lists_hbm, lraw, load_sem.at[5]),
    ]
    for load in loads:
        load.start()

    barrier = pltpu.get_barrier_semaphore()

    def peer(i, sign):
        dx, dy = lax.rem(i, side), lax.rem(i + i // side, side)
        x = lax.rem(view // side + sign * dx + side, side)
        y = lax.rem(lax.rem(view, side) + sign * dy + side, side)
        return x * side + y

    def greet_view(i, c):
        pl.semaphore_signal(barrier, inc=1, device_id=(peer(i, 1), tok), device_id_type=MESH)
        return c

    def greet_tok(i, c):
        pl.semaphore_signal(
            barrier, inc=1, device_id=(view, lax.rem(tok + i, ntok)), device_id_type=MESH
        )
        return c

    lax.fori_loop(1, nview, greet_view, 0)
    lax.fori_loop(1, ntok, greet_tok, 0)

    low = lax.broadcasted_iota(jnp.int32, (1, 2 * HD), 1) < HD

    def split(x, count):
        x = x.reshape(count, 2, -1, 2 * HD)
        first = x[:, 0].reshape(-1, 2 * HD)
        second = pltpu.roll(x[:, 1].reshape(-1, 2 * HD), HD, 1)
        even = jnp.where(low, first, second).astype(jnp.bfloat16)
        odd = jnp.where(low, second, first).astype(jnp.bfloat16)
        return even, odd

    def project_q(j, c):
        columns = pl.ds(pl.multiple_of(j * 256, 256), 256)
        query = dot(xall[pl.ds(0, rows), :], wq[:, columns])
        for p in range(2):
            even, odd = split(query[:, p * 128 : (p + 1) * 128], 1)
            qsend[4 * j + 2 * p] = even
            qsend[4 * j + 2 * p + 1] = odd
        return c

    loads[0].wait()
    loads[1].wait()
    lax.fori_loop(0, width // 256, project_q, 0)

    pl.semaphore_wait(barrier, nview + ntok - 2)

    def view_copy(i, name):
        to = peer(i, 1)
        target = (to, tok)

        def remote(src, dst, send, recv, at):
            return pltpu.make_async_remote_copy(
                src_ref=src, dst_ref=dst, send_sem=send.at[at], recv_sem=recv.at[at],
                device_id=target, device_id_type=MESH,
            )

        own = pl.ds((nview + view) * nblk, nblk)
        if name == "c":
            return remote(csend.at[to], condkv.at[tok, view], c_ss, c_rs, i)
        if name == "l":
            return remote(lsend, lists_v.at[view], l_ss, l_rs, i)
        if name == "q":
            return remote(qsend.at[to], qrecv.at[view], q_ss, q_rs, i)
        if name == "k":
            return remote(ksend.at[to], kpool.at[own], kv_ss, kv_rs, i)
        return remote(vsend.at[to], vpool.at[own], kv_ss, kv_rs, nview + i)

    def start(*names, lo=1, hi=nview):
        def body(i, c):
            for name in names:
                view_copy(i, name).start()
            return c

        lax.fori_loop(lo, hi, body, 0)

    start("q", hi=1 + FIRST)
    for load in loads[2:]:
        load.wait()

    def project_kv(j, c):
        columns = pl.ds(pl.multiple_of(j * 256, 256), 256)
        keys = dot(xall[...], wk[:, columns])
        values = dot(xall[...], wv[:, columns])
        for p in range(2):
            head = 4 * j + 2 * p
            k = keys[:, p * 128 : (p + 1) * 128]
            v = values[:, p * 128 : (p + 1) * 128]
            for send, x in ((ksend, k), (vsend, v)):
                even, odd = split(x[:rows], nblk)
                send[head] = even.reshape(nblk, BLK // 2, 2 * HD)
                send[head + 1] = odd.reshape(nblk, BLK // 2, 2 * HD)
            k, v = k[rows:], pltpu.roll(v[rows:], HD, 1)
            csend[head] = jnp.where(low, k, v).astype(jnp.bfloat16)
            csend[head + 1] = jnp.where(low, v, k).astype(jnp.bfloat16)
        return c

    lax.fori_loop(0, width // 256, project_kv, 0)
    raw = lraw[...]
    entry_view, entry_block = raw[:, 0, :], raw[:, 1, :] - (tok - 1) * nblk
    band, inner = entry_block // nblk, lax.rem(entry_block, nblk)
    place = (band * nview + entry_view) * nblk + inner
    place = jnp.where(entry_view >= 0, place, 3 * nview * nblk)
    place = jnp.clip(place, 0, 3 * nview * nblk)
    lsend[...] = jnp.zeros((8, 128), jnp.int32)
    lsend[pl.ds(0, nblk), pl.ds(0, most)] = place
    start("c", "l")
    start("q", lo=1 + FIRST)
    start("k", "v")
    condkv[tok, view] = csend[view]
    lists_v[view] = lsend[...]
    qrecv[view] = qsend[view]
    kpool[pl.ds((nview + view) * nblk, nblk)] = ksend[view]
    vpool[pl.ds((nview + view) * nblk, nblk)] = vsend[view]

    def wait_view(name, start_i=1):
        def body(i, c):
            view_copy(i, name).wait_recv()
            return c

        lax.fori_loop(start_i, nview, body, 0)

    wait_view("c")

    def tok_copy(i):
        return pltpu.make_async_remote_copy(
            src_ref=condkv.at[tok], dst_ref=condkv.at[tok],
            send_sem=g_ss.at[i], recv_sem=g_rs.at[i],
            device_id=(view, lax.rem(tok + i, ntok)), device_id_type=MESH,
        )

    def start_tok(i, c):
        tok_copy(i).start()
        return c

    def wait_tok(i, c):
        tok_copy(i).wait_recv()
        return c

    lax.fori_loop(1, ntok, start_tok, 0)
    lax.fori_loop(1, ntok, wait_tok, 0)

    parity = lax.rem(view, 2)
    lane = lax.broadcasted_iota(jnp.int32, (1, 2 * HD), 1)
    khalf = (lane // HD) == parity
    kf = jnp.where(khalf, 1.0, 0.0)
    krow = kf.astype(jnp.bfloat16)
    vrow = (1.0 - kf).astype(jnp.bfloat16)
    count = ntok * nview * crows

    spare = condkv[0, pl.ds(0, BLK // crows)].reshape(BLK, 2 * HD).astype(jnp.float32)
    kpool[3 * nview * nblk] = jnp.where(
        khalf, spare[: BLK // 2], pltpu.roll(spare[BLK // 2 :], HD, 1)
    ).astype(jnp.bfloat16)
    vpool[3 * nview * nblk] = jnp.zeros((BLK // 2, 2 * HD), jnp.bfloat16)
    vcond[...] = condkv[...].reshape(count, 2 * HD) * vrow + krow

    def forward(i, part, direction):
        owner = peer(i, -1) * nblk
        pool = (kpool, vpool)[part]
        step = 1 if direction == 0 else ntok - 1
        sem = part * nview + i
        return pltpu.make_async_remote_copy(
            src_ref=pool.at[pl.ds(nview * nblk + owner, nblk)],
            dst_ref=pool.at[pl.ds(2 * direction * nview * nblk + owner, nblk)],
            send_sem=f_ss.at[direction, sem], recv_sem=f_rs.at[direction, sem],
            device_id=(view, lax.rem(tok + step, ntok)), device_id_type=MESH,
        )

    for part in range(2):
        forward(0, part, 0).start()
        forward(0, part, 1).start()

    def pass_on(i):
        for part, name in enumerate("kv"):
            view_copy(i, name).wait_recv()
            forward(i, part, 0).start()
            forward(i, part, 1).start()

    def cond_step(i, c):
        @pl.when(i > 0)
        def _():
            view_copy(i, "q").wait_recv()

        packed = qrecv[peer(i, -1)].astype(jnp.float32)
        rolled = pltpu.roll(packed, HD, 1)
        first = [
            jnp.where(khalf, packed, 0.0).astype(jnp.bfloat16),
            jnp.where(khalf, rolled, 0.0).astype(jnp.bfloat16),
        ]
        other = [
            jnp.where(khalf, 0.0, rolled).astype(jnp.bfloat16),
            jnp.where(khalf, 0.0, packed).astype(jnp.bfloat16),
        ]
        ck = condkv[...].reshape(count, 2 * HD)
        scores = [dot_t(first[part], ck) for part in range(2)]
        for part in range(2):
            peak = jnp.max(scores[part], axis=1, keepdims=True)
            weights = jnp.exp2((scores[part] - peak) * scale).astype(jnp.bfloat16)
            total = dot(weights, vcond[...])
            peak = jnp.broadcast_to(peak, (half, 2 * HD))
            for b in range(nblk // 2):
                at = slice(b * BLK, (b + 1) * BLK)
                to = part * (nblk // 2) + b
                qstk[i, to, pl.ds(0, BLK)] = first[part][at]
                qstk[i, to, pl.ds(BLK, BLK)] = other[part][at]
                turned = total[at].T
                acc_t[i, to, pl.ds(0, HD)] = jnp.where(parity == 0, turned[HD:], turned[:HD])
                acc_t[i, to, pl.ds(HD, 8)] = jnp.where(
                    parity == 0, turned[:8], turned[HD : HD + 8]
                )
                peak_t[i, to] = peak[at].T[:8]

        @pl.when(i > LAG)
        def _():
            pass_on(i - LAG)

        return c

    lax.fori_loop(0, nview, cond_step, 0)

    def rest(i, c):
        pass_on(i)
        return c

    lax.fori_loop(nview - LAG, nview, rest, 0)
    wait_view("l")
    to_smem = pltpu.make_async_copy(lists_v, lists_s, smem_sem)
    to_smem.start()
    to_smem.wait()

    def wait_forward(i, c):
        for part in range(2):
            forward(i, part, 0).wait_recv()
            forward(i, part, 1).wait_recv()
        return c

    lax.fori_loop(0, nview, wait_forward, 0)

    def o_copy(i):
        return pltpu.make_async_remote_copy(
            src_ref=osend.at[i], dst_ref=orecv.at[view],
            send_sem=o_ss.at[i], recv_sem=o_rs.at[i],
            device_id=(peer(i, -1), tok), device_id_type=MESH,
        )

    half_lane = lane < HD

    def epi_step(j, c):
        steps = [lax.rem(VPS * j + a + 1, nview) for a in range(VPS)]
        work = [(i, peer(i, -1), b) for i in steps for b in range(nblk)]
        unused = 3 * nview * nblk
        scores, parts = [], []
        for i, owner, b in work:
            keys = jnp.concatenate([kpool[lists_s[owner, b, s]] for s in range(most)], axis=0)
            scores.append(dot_t(keys, qstk[i, b]))
        for (i, owner, b), score in zip(work, scores):
            before = peak_t[i, b][:1]
            peak = jnp.max(score, axis=0, keepdims=True)
            peak = jnp.maximum(jnp.maximum(peak[:, :BLK], peak[:, BLK:]), before)
            weights = jnp.exp2((score - jnp.concatenate([peak, peak], axis=1)) * scale)
            weights = weights.astype(jnp.bfloat16)
            fade = jnp.exp2((before - peak) * scale)
            entries = [lists_s[owner, b, s] for s in range(most)]
            used = [jnp.where(entry < unused, 1.0, 0.0) for entry in entries]
            values = jnp.concatenate([vpool[entry] for entry in entries], axis=0)
            sums = jnp.concatenate(
                [
                    jnp.broadcast_to(jnp.where(half_lane, used[s], used[s + 1]), (16, 2 * HD))
                    for s in range(0, most, 2)
                ],
                axis=1,
            ).astype(jnp.bfloat16)
            top = lax.dot_general(
                values, weights, (((0,), (0,)), ((), ())), preferred_element_type=jnp.float32
            )
            ones = dot(sums, weights)
            part = jnp.where(
                parity == 0,
                top[:HD, :BLK] + top[HD:, BLK:],
                top[HD:, :BLK] + top[:HD, BLK:],
            )
            total = ones[:1, :BLK] + ones[:1, BLK:] + acc_t[i, b, pl.ds(HD, 8)][:1] * fade
            parts.append((part + acc_t[i, b, pl.ds(0, HD)] * fade) / total)
        for a, i in enumerate(steps):
            mine = parts[a * nblk : (a + 1) * nblk]
            for b in range(nblk // 2):
                pair = jnp.concatenate([mine[b], mine[b + nblk // 2]], axis=0)
                osend[i, pl.ds(b * BLK, BLK)] = pair.T.astype(jnp.bfloat16)
            if a < VPS - 1:
                o_copy(i).start()
            else:

                @pl.when(i > 0)
                def _():
                    o_copy(i).start()

                @pl.when(i == 0)
                def _():
                    orecv[view] = osend[i]

        return c

    lax.fori_loop(0, nview // VPS, epi_step, 0)

    def wait_o(i, c):
        o_copy(i).wait_recv()
        return c

    lax.fori_loop(1, nview, wait_o, 0)

    for j in range(nview // 2):
        even = orecv[2 * j].astype(jnp.float32)
        odd = orecv[2 * j + 1].astype(jnp.float32)
        at = pl.ds(j * 128, 128)
        att[pl.ds(0, half), at] = jnp.where(low, even, pltpu.roll(odd, HD, 1)).astype(jnp.bfloat16)
        att[pl.ds(half, half), at] = jnp.where(low, pltpu.roll(even, HD, 1), odd).astype(
            jnp.bfloat16
        )

    store = pltpu.make_async_copy(att, out_hbm, out_sem)
    store.start()

    def wait_sends(i, c):
        for name in ("c", "l", "q", "k", "v"):
            view_copy(i, name).wait_send()
        o_copy(i).wait_send()
        return c

    def wait_tok_sends(i, c):
        tok_copy(i).wait_send()
        return c

    def wait_forward_sends(i, c):
        for part in range(2):
            forward(i, part, 0).wait_send()
            forward(i, part, 1).wait_send()
        return c

    lax.fori_loop(1, nview, wait_sends, 0)
    lax.fori_loop(1, ntok, wait_tok_sends, 0)
    lax.fori_loop(0, nview, wait_forward_sends, 0)
    store.wait()


def local(x_target, cond_x, w_query, w_key, w_value, w_out, epi_lists):
    nview = lax.axis_size("view")
    ntok = lax.axis_size("tok")
    rows, width = x_target.shape[1:]
    crows = cond_x.shape[0]
    most = epi_lists.shape[2]
    nblk = rows // BLK
    lists = jnp.transpose(epi_lists[0], (0, 2, 1))
    bf, f32 = jnp.bfloat16, jnp.float32
    half = rows // 2
    dma = pltpu.SemaphoreType.DMA
    scratch = [
        pltpu.VMEM((rows + crows, width), bf),
        pltpu.VMEM((width, width), bf),
        pltpu.VMEM((width, width), bf),
        pltpu.VMEM((width, width), bf),
        pltpu.VMEM((nview, half, 128), bf),
        pltpu.VMEM((nview, nblk, BLK // 2, 128), bf),
        pltpu.VMEM((nview, nblk, BLK // 2, 128), bf),
        pltpu.VMEM((nview, crows, 128), bf),
        pltpu.VMEM((nblk, 2, most), jnp.int32),
        pltpu.VMEM((8, 128), jnp.int32),
        pltpu.VMEM((nview, half, 128), bf),
        pltpu.VMEM((3 * nview * nblk + 1, BLK // 2, 128), bf),
        pltpu.VMEM((3 * nview * nblk + 1, BLK // 2, 128), bf),
        pltpu.VMEM((ntok, nview, crows, 128), bf),
        pltpu.VMEM((nview, 8, 128), jnp.int32),
        pltpu.SMEM((nview, 8, 128), jnp.int32),
        pltpu.VMEM((ntok * nview * crows, 128), bf),
        pltpu.VMEM((nview, nblk, 2 * BLK, 128), bf),
        pltpu.VMEM((nview, nblk, HD + 8, BLK), f32),
        pltpu.VMEM((nview, nblk, 8, BLK), f32),
        pltpu.VMEM((nview, half, 128), bf),
        pltpu.VMEM((nview, half, 128), bf),
        pltpu.VMEM((rows, width), bf),
        dma((6,)),
        dma((nview,)), dma((nview,)),
        dma((2 * nview,)), dma((2 * nview,)),
        *[dma((nview,)) for _ in range(4)],
        dma((ntok,)), dma((ntok,)),
        dma((2, 2 * nview)), dma((2, 2 * nview)),
        dma((nview,)), dma((nview,)),
        dma, dma,
    ]
    attended = pl.pallas_call(
        functools.partial(kernel, nview, ntok, math.isqrt(nview), rows, crows, most),
        out_shape=jax.ShapeDtypeStruct((rows, width), bf),
        in_specs=[pl.BlockSpec(memory_space=pl.ANY)] * 6,
        out_specs=pl.BlockSpec(memory_space=pl.ANY),
        scratch_shapes=scratch,
        compiler_params=pltpu.CompilerParams(
            collective_id=0, has_side_effects=True, vmem_limit_bytes=60 * 1024 * 1024
        ),
    )(x_target[0], cond_x, w_query, w_key, w_value, lists)
    return dot(attended, w_out).astype(bf)[None]


def solution(mesh):
    placed = (
        P("view", "tok", None),
        P(("view", "tok"), None),
        P(),
        P(),
        P(),
        P(),
        P("view", "tok", None, None),
    )
    return jax.shard_map(
        local, mesh=mesh, in_specs=placed, out_specs=P("view", "tok", None), check_vma=False
    )
```

```python
import functools
import math

import jax
import jax.numpy as jnp
from jax import lax
from jax.experimental import pallas as pl
from jax.experimental.pallas import tpu as pltpu
from jax.sharding import PartitionSpec as P

HD = 64
BLK = 128
MESH = pl.DeviceIdType.MESH
LAG = 2
FIRST = 7
VPS = 2


def dot(a, b):
    return jnp.dot(a, b, preferred_element_type=jnp.float32)


def dot_t(a, b):
    return lax.dot_general(a, b, (((1,), (1,)), ((), ())), preferred_element_type=jnp.float32)


def kernel(
    nview, ntok, side, rows, crows, most,
    x_hbm, cond_hbm, wq_hbm, wk_hbm, wv_hbm, lists_hbm,
    out_hbm,
    xall, wq, wk, wv,
    qsend, ksend, vsend, csend, lraw, lsend,
    qrecv, kpool, vpool, condkv, lists_v, lists_s,
    vcond, qstk, acc_t, peak_t, osend, orecv, att,
    load_sem, q_ss, q_rs, kv_ss, kv_rs, c_ss, c_rs, l_ss, l_rs, g_ss, g_rs, f_ss, f_rs, o_ss, o_rs, smem_sem, out_sem,
):
    view = lax.axis_index("view")
    tok = lax.axis_index("tok")
    width = nview * HD
    half = rows // 2
    nblk = rows // BLK
    scale = math.log2(math.e) * HD ** -0.5

    loads = [
        pltpu.make_async_copy(x_hbm, xall.at[pl.ds(0, rows)], load_sem.at[0]),
        pltpu.make_async_copy(wq_hbm, wq, load_sem.at[1]),
        pltpu.make_async_copy(cond_hbm, xall.at[pl.ds(rows, crows)], load_sem.at[2]),
        pltpu.make_async_copy(wk_hbm, wk, load_sem.at[3]),
        pltpu.make_async_copy(wv_hbm, wv, load_sem.at[4]),
        pltpu.make_async_copy(lists_hbm, lraw, load_sem.at[5]),
    ]
    for load in loads:
        load.start()

    barrier = pltpu.get_barrier_semaphore()

    def peer(i, sign):
        dx, dy = lax.rem(i, side), lax.rem(i + i // side, side)
        x = lax.rem(view // side + sign * dx + side, side)
        y = lax.rem(lax.rem(view, side) + sign * dy + side, side)
        return x * side + y

    def greet_view(i, c):
        pl.semaphore_signal(barrier, inc=1, device_id=(peer(i, 1), tok), device_id_type=MESH)
        return c

    def greet_tok(i, c):
        pl.semaphore_signal(
            barrier, inc=1, device_id=(view, lax.rem(tok + i, ntok)), device_id_type=MESH
        )
        return c

    lax.fori_loop(1, nview, greet_view, 0)
    lax.fori_loop(1, ntok, greet_tok, 0)

    low = lax.broadcasted_iota(jnp.int32, (1, 2 * HD), 1) < HD

    def split(x, count):
        x = x.reshape(count, 2, -1, 2 * HD)
        first = x[:, 0].reshape(-1, 2 * HD)
        second = pltpu.roll(x[:, 1].reshape(-1, 2 * HD), HD, 1)
        even = jnp.where(low, first, second).astype(jnp.bfloat16)
        odd = jnp.where(low, second, first).astype(jnp.bfloat16)
        return even, odd

    def project_q(j, c):
        columns = pl.ds(pl.multiple_of(j * 256, 256), 256)
        query = dot(xall[pl.ds(0, rows), :], wq[:, columns])
        for p in range(2):
            even, odd = split(query[:, p * 128 : (p + 1) * 128], 1)
            qsend[4 * j + 2 * p] = even
            qsend[4 * j + 2 * p + 1] = odd
        return c

    loads[0].wait()
    loads[1].wait()
    lax.fori_loop(0, width // 256, project_q, 0)

    pl.semaphore_wait(barrier, nview + ntok - 2)

    def view_copy(i, name):
        to = peer(i, 1)
        target = (to, tok)

        def remote(src, dst, send, recv, at):
            return pltpu.make_async_remote_copy(
                src_ref=src, dst_ref=dst, send_sem=send.at[at], recv_sem=recv.at[at],
                device_id=target, device_id_type=MESH,
            )

        own = pl.ds((nview + view) * nblk, nblk)
        if name == "c":
            return remote(csend.at[to], condkv.at[tok, view], c_ss, c_rs, i)
        if name == "l":
            return remote(lsend, lists_v.at[view], l_ss, l_rs, i)
        if name == "q":
            return remote(qsend.at[to], qrecv.at[view], q_ss, q_rs, i)
        if name == "k":
            return remote(ksend.at[to], kpool.at[own], kv_ss, kv_rs, i)
        return remote(vsend.at[to], vpool.at[own], kv_ss, kv_rs, nview + i)

    def start(*names, lo=1, hi=nview):
        def body(i, c):
            for name in names:
                view_copy(i, name).start()
            return c

        lax.fori_loop(lo, hi, body, 0)

    start("q", hi=1 + FIRST)
    for load in loads[2:]:
        load.wait()

    def project_kv(j, c):
        columns = pl.ds(pl.multiple_of(j * 256, 256), 256)
        keys = dot(xall[...], wk[:, columns])
        values = dot(xall[...], wv[:, columns])
        for p in range(2):
            head = 4 * j + 2 * p
            k = keys[:, p * 128 : (p + 1) * 128]
            v = values[:, p * 128 : (p + 1) * 128]
            for send, x in ((ksend, k), (vsend, v)):
                even, odd = split(x[:rows], nblk)
                send[head] = even.reshape(nblk, BLK // 2, 2 * HD)
                send[head + 1] = odd.reshape(nblk, BLK // 2, 2 * HD)
            k, v = k[rows:], pltpu.roll(v[rows:], HD, 1)
            csend[head] = jnp.where(low, k, v).astype(jnp.bfloat16)
            csend[head + 1] = jnp.where(low, v, k).astype(jnp.bfloat16)
        return c

    lax.fori_loop(0, width // 256, project_kv, 0)
    raw = lraw[...]
    entry_view, entry_block = raw[:, 0, :], raw[:, 1, :] - (tok - 1) * nblk
    band, inner = entry_block // nblk, lax.rem(entry_block, nblk)
    place = (band * nview + entry_view) * nblk + inner
    place = jnp.where(entry_view >= 0, place, 3 * nview * nblk)
    place = jnp.clip(place, 0, 3 * nview * nblk)
    lsend[...] = jnp.zeros((8, 128), jnp.int32)
    lsend[pl.ds(0, nblk), pl.ds(0, most)] = place
    start("c", "l")
    start("q", lo=1 + FIRST)
    start("k", "v")
    condkv[tok, view] = csend[view]
    lists_v[view] = lsend[...]
    qrecv[view] = qsend[view]
    kpool[pl.ds((nview + view) * nblk, nblk)] = ksend[view]
    vpool[pl.ds((nview + view) * nblk, nblk)] = vsend[view]

    def wait_view(name, start_i=1):
        def body(i, c):
            view_copy(i, name).wait_recv()
            return c

        lax.fori_loop(start_i, nview, body, 0)

    wait_view("c")

    def tok_copy(i):
        return pltpu.make_async_remote_copy(
            src_ref=condkv.at[tok], dst_ref=condkv.at[tok],
            send_sem=g_ss.at[i], recv_sem=g_rs.at[i],
            device_id=(view, lax.rem(tok + i, ntok)), device_id_type=MESH,
        )

    def start_tok(i, c):
        tok_copy(i).start()
        return c

    def wait_tok(i, c):
        tok_copy(i).wait_recv()
        return c

    lax.fori_loop(1, ntok, start_tok, 0)
    lax.fori_loop(1, ntok, wait_tok, 0)

    parity = lax.rem(view, 2)
    lane = lax.broadcasted_iota(jnp.int32, (1, 2 * HD), 1)
    khalf = (lane // HD) == parity
    kf = jnp.where(khalf, 1.0, 0.0)
    krow = kf.astype(jnp.bfloat16)
    vrow = (1.0 - kf).astype(jnp.bfloat16)
    count = ntok * nview * crows

    spare = condkv[0, pl.ds(0, BLK // crows)].reshape(BLK, 2 * HD).astype(jnp.float32)
    kpool[3 * nview * nblk] = jnp.where(
        khalf, spare[: BLK // 2], pltpu.roll(spare[BLK // 2 :], HD, 1)
    ).astype(jnp.bfloat16)
    vpool[3 * nview * nblk] = jnp.zeros((BLK // 2, 2 * HD), jnp.bfloat16)
    vcond[...] = condkv[...].reshape(count, 2 * HD) * vrow + krow

    def forward(i, part, direction):
        owner = peer(i, -1) * nblk
        pool = (kpool, vpool)[part]
        step = 1 if direction == 0 else ntok - 1
        sem = part * nview + i
        return pltpu.make_async_remote_copy(
            src_ref=pool.at[pl.ds(nview * nblk + owner, nblk)],
            dst_ref=pool.at[pl.ds(2 * direction * nview * nblk + owner, nblk)],
            send_sem=f_ss.at[direction, sem], recv_sem=f_rs.at[direction, sem],
            device_id=(view, lax.rem(tok + step, ntok)), device_id_type=MESH,
        )

    for part in range(2):
        forward(0, part, 0).start()
        forward(0, part, 1).start()

    def pass_on(i):
        for part, name in enumerate("kv"):
            view_copy(i, name).wait_recv()
            forward(i, part, 0).start()
            forward(i, part, 1).start()

    def cond_step(i, c):
        @pl.when(i > 0)
        def _():
            view_copy(i, "q").wait_recv()

        packed = qrecv[peer(i, -1)].astype(jnp.float32)
        rolled = pltpu.roll(packed, HD, 1)
        first = [
            jnp.where(khalf, packed, 0.0).astype(jnp.bfloat16),
            jnp.where(khalf, rolled, 0.0).astype(jnp.bfloat16),
        ]
        other = [
            jnp.where(khalf, 0.0, rolled).astype(jnp.bfloat16),
            jnp.where(khalf, 0.0, packed).astype(jnp.bfloat16),
        ]
        ck = condkv[...].reshape(count, 2 * HD)
        scores = [dot_t(first[part], ck) for part in range(2)]
        for part in range(2):
            peak = jnp.max(scores[part], axis=1, keepdims=True)
            weights = jnp.exp2((scores[part] - peak) * scale).astype(jnp.bfloat16)
            total = dot(weights, vcond[...])
            peak = jnp.broadcast_to(peak, (half, 2 * HD))
            for b in range(nblk // 2):
                at = slice(b * BLK, (b + 1) * BLK)
                to = part * (nblk // 2) + b
                qstk[i, to, pl.ds(0, BLK)] = first[part][at]
                qstk[i, to, pl.ds(BLK, BLK)] = other[part][at]
                turned = total[at].T
                acc_t[i, to, pl.ds(0, HD)] = jnp.where(parity == 0, turned[HD:], turned[:HD])
                acc_t[i, to, pl.ds(HD, 8)] = jnp.where(
                    parity == 0, turned[:8], turned[HD : HD + 8]
                )
                peak_t[i, to] = peak[at].T[:8]

        @pl.when(i > LAG)
        def _():
            pass_on(i - LAG)

        return c

    lax.fori_loop(0, nview, cond_step, 0)

    def rest(i, c):
        pass_on(i)
        return c

    lax.fori_loop(nview - LAG, nview, rest, 0)
    wait_view("l")
    to_smem = pltpu.make_async_copy(lists_v, lists_s, smem_sem)
    to_smem.start()
    to_smem.wait()

    def wait_forward(i, c):
        for part in range(2):
            forward(i, part, 0).wait_recv()
            forward(i, part, 1).wait_recv()
        return c

    lax.fori_loop(0, nview, wait_forward, 0)

    def o_copy(i):
        return pltpu.make_async_remote_copy(
            src_ref=osend.at[i], dst_ref=orecv.at[view],
            send_sem=o_ss.at[i], recv_sem=o_rs.at[i],
            device_id=(peer(i, -1), tok), device_id_type=MESH,
        )

    half_lane = lane < HD

    def epi_step(j, c):
        steps = [lax.rem(VPS * j + a + 1, nview) for a in range(VPS)]
        work = [(i, peer(i, -1), b) for i in steps for b in range(nblk)]
        unused = 3 * nview * nblk
        scores, parts = [], []
        for i, owner, b in work:
            keys = jnp.concatenate([kpool[lists_s[owner, b, s]] for s in range(most)], axis=0)
            scores.append(dot_t(keys, qstk[i, b]))
        for (i, owner, b), score in zip(work, scores):
            before = peak_t[i, b][:1]
            peak = jnp.max(score, axis=0, keepdims=True)
            peak = jnp.maximum(jnp.maximum(peak[:, :BLK], peak[:, BLK:]), before)
            weights = jnp.exp2((score - jnp.concatenate([peak, peak], axis=1)) * scale)
            weights = weights.astype(jnp.bfloat16)
            fade = jnp.exp2((before - peak) * scale)
            entries = [lists_s[owner, b, s] for s in range(most)]
            used = [jnp.where(entry < unused, 1.0, 0.0) for entry in entries]
            values = jnp.concatenate([vpool[entry] for entry in entries], axis=0)
            sums = jnp.concatenate(
                [
                    jnp.broadcast_to(jnp.where(half_lane, used[s], used[s + 1]), (16, 2 * HD))
                    for s in range(0, most, 2)
                ],
                axis=1,
            ).astype(jnp.bfloat16)
            both = dot(jnp.concatenate([values.T, sums], axis=0), weights)
            top, ones = both[: 2 * HD], both[2 * HD :]
            part = jnp.where(
                parity == 0,
                top[:HD, :BLK] + top[HD:, BLK:],
                top[HD:, :BLK] + top[:HD, BLK:],
            )
            total = ones[:1, :BLK] + ones[:1, BLK:] + acc_t[i, b, pl.ds(HD, 8)][:1] * fade
            parts.append((part + acc_t[i, b, pl.ds(0, HD)] * fade) / total)
        for a, i in enumerate(steps):
            mine = parts[a * nblk : (a + 1) * nblk]
            for b in range(nblk // 2):
                pair = jnp.concatenate([mine[b], mine[b + nblk // 2]], axis=0)
                osend[i, pl.ds(b * BLK, BLK)] = pair.T.astype(jnp.bfloat16)
            if a < VPS - 1:
                o_copy(i).start()
            else:

                @pl.when(i > 0)
                def _():
                    o_copy(i).start()

                @pl.when(i == 0)
                def _():
                    orecv[view] = osend[i]

        return c

    lax.fori_loop(0, nview // VPS, epi_step, 0)

    def wait_o(i, c):
        o_copy(i).wait_recv()
        return c

    lax.fori_loop(1, nview, wait_o, 0)

    for j in range(nview // 2):
        even = orecv[2 * j].astype(jnp.float32)
        odd = orecv[2 * j + 1].astype(jnp.float32)
        at = pl.ds(j * 128, 128)
        att[pl.ds(0, half), at] = jnp.where(low, even, pltpu.roll(odd, HD, 1)).astype(jnp.bfloat16)
        att[pl.ds(half, half), at] = jnp.where(low, pltpu.roll(even, HD, 1), odd).astype(
            jnp.bfloat16
        )

    store = pltpu.make_async_copy(att, out_hbm, out_sem)
    store.start()

    def wait_sends(i, c):
        for name in ("c", "l", "q", "k", "v"):
            view_copy(i, name).wait_send()
        o_copy(i).wait_send()
        return c

    def wait_tok_sends(i, c):
        tok_copy(i).wait_send()
        return c

    def wait_forward_sends(i, c):
        for part in range(2):
            forward(i, part, 0).wait_send()
            forward(i, part, 1).wait_send()
        return c

    lax.fori_loop(1, nview, wait_sends, 0)
    lax.fori_loop(1, ntok, wait_tok_sends, 0)
    lax.fori_loop(0, nview, wait_forward_sends, 0)
    store.wait()


def local(x_target, cond_x, w_query, w_key, w_value, w_out, epi_lists):
    nview = lax.axis_size("view")
    ntok = lax.axis_size("tok")
    rows, width = x_target.shape[1:]
    crows = cond_x.shape[0]
    most = epi_lists.shape[2]
    nblk = rows // BLK
    lists = jnp.transpose(epi_lists[0], (0, 2, 1))
    bf, f32 = jnp.bfloat16, jnp.float32
    half = rows // 2
    dma = pltpu.SemaphoreType.DMA
    scratch = [
        pltpu.VMEM((rows + crows, width), bf),
        pltpu.VMEM((width, width), bf),
        pltpu.VMEM((width, width), bf),
        pltpu.VMEM((width, width), bf),
        pltpu.VMEM((nview, half, 128), bf),
        pltpu.VMEM((nview, nblk, BLK // 2, 128), bf),
        pltpu.VMEM((nview, nblk, BLK // 2, 128), bf),
        pltpu.VMEM((nview, crows, 128), bf),
        pltpu.VMEM((nblk, 2, most), jnp.int32),
        pltpu.VMEM((8, 128), jnp.int32),
        pltpu.VMEM((nview, half, 128), bf),
        pltpu.VMEM((3 * nview * nblk + 1, BLK // 2, 128), bf),
        pltpu.VMEM((3 * nview * nblk + 1, BLK // 2, 128), bf),
        pltpu.VMEM((ntok, nview, crows, 128), bf),
        pltpu.VMEM((nview, 8, 128), jnp.int32),
        pltpu.SMEM((nview, 8, 128), jnp.int32),
        pltpu.VMEM((ntok * nview * crows, 128), bf),
        pltpu.VMEM((nview, nblk, 2 * BLK, 128), bf),
        pltpu.VMEM((nview, nblk, HD + 8, BLK), f32),
        pltpu.VMEM((nview, nblk, 8, BLK), f32),
        pltpu.VMEM((nview, half, 128), bf),
        pltpu.VMEM((nview, half, 128), bf),
        pltpu.VMEM((rows, width), bf),
        dma((6,)),
        dma((nview,)), dma((nview,)),
        dma((2 * nview,)), dma((2 * nview,)),
        *[dma((nview,)) for _ in range(4)],
        dma((ntok,)), dma((ntok,)),
        dma((2, 2 * nview)), dma((2, 2 * nview)),
        dma((nview,)), dma((nview,)),
        dma, dma,
    ]
    attended = pl.pallas_call(
        functools.partial(kernel, nview, ntok, math.isqrt(nview), rows, crows, most),
        out_shape=jax.ShapeDtypeStruct((rows, width), bf),
        in_specs=[pl.BlockSpec(memory_space=pl.ANY)] * 6,
        out_specs=pl.BlockSpec(memory_space=pl.ANY),
        scratch_shapes=scratch,
        compiler_params=pltpu.CompilerParams(
            collective_id=0, has_side_effects=True, vmem_limit_bytes=60 * 1024 * 1024
        ),
    )(x_target[0], cond_x, w_query, w_key, w_value, lists)
    return dot(attended, w_out).astype(bf)[None]


def solution(mesh):
    placed = (
        P("view", "tok", None),
        P(("view", "tok"), None),
        P(),
        P(),
        P(),
        P(),
        P("view", "tok", None, None),
    )
    return jax.shard_map(
        local, mesh=mesh, in_specs=placed, out_specs=P("view", "tok", None), check_vma=False
    )
```

```python
import functools
import math

import jax
import jax.numpy as jnp
from jax import lax
from jax.experimental import pallas as pl
from jax.experimental.pallas import tpu as pltpu
from jax.sharding import PartitionSpec as P

HD = 64
BLK = 128
MESH = pl.DeviceIdType.MESH
LAG = 1
FIRST = 7
VPS = 2


def dot(a, b):
    return jnp.dot(a, b, preferred_element_type=jnp.float32)


def dot_t(a, b):
    return lax.dot_general(a, b, (((1,), (1,)), ((), ())), preferred_element_type=jnp.float32)


def kernel(
    nview, ntok, side, rows, crows, most,
    x_hbm, cond_hbm, wq_hbm, wk_hbm, wv_hbm, lists_hbm,
    out_hbm,
    xall, wq, wk, wv,
    qsend, kvsend, csend, lraw, lsend,
    qrecv, pool, condkv, lists_v, lists_s,
    vcond, qstk, acc_t, peak_t, osend, orecv, att,
    load_sem, q_ss, q_rs, kv_ss, kv_rs, c_ss, c_rs, l_ss, l_rs, g_ss, g_rs, f_ss, f_rs, o_ss, o_rs, smem_sem, out_sem,
):
    view = lax.axis_index("view")
    tok = lax.axis_index("tok")
    width = nview * HD
    half = rows // 2
    nblk = rows // BLK
    scale = math.log2(math.e) * HD ** -0.5
    unused = 3 * nview * 2 * nblk

    loads = [
        pltpu.make_async_copy(x_hbm, xall.at[pl.ds(0, rows)], load_sem.at[0]),
        pltpu.make_async_copy(wq_hbm, wq, load_sem.at[1]),
        pltpu.make_async_copy(cond_hbm, xall.at[pl.ds(rows, crows)], load_sem.at[2]),
        pltpu.make_async_copy(wk_hbm, wk, load_sem.at[3]),
        pltpu.make_async_copy(wv_hbm, wv, load_sem.at[4]),
        pltpu.make_async_copy(lists_hbm, lraw, load_sem.at[5]),
    ]
    for load in loads:
        load.start()

    barrier = pltpu.get_barrier_semaphore()

    def peer(i, sign):
        dx, dy = lax.rem(i, side), lax.rem(i + i // side, side)
        x = lax.rem(view // side + sign * dx + side, side)
        y = lax.rem(lax.rem(view, side) + sign * dy + side, side)
        return x * side + y

    def greet_view(i, c):
        pl.semaphore_signal(barrier, inc=1, device_id=(peer(i, 1), tok), device_id_type=MESH)
        return c

    def greet_tok(i, c):
        pl.semaphore_signal(
            barrier, inc=1, device_id=(view, lax.rem(tok + i, ntok)), device_id_type=MESH
        )
        return c

    lax.fori_loop(1, nview, greet_view, 0)
    lax.fori_loop(1, ntok, greet_tok, 0)

    low = lax.broadcasted_iota(jnp.int32, (1, 2 * HD), 1) < HD

    def split(x, count):
        x = x.reshape(count, 2, -1, 2 * HD)
        first = x[:, 0].reshape(-1, 2 * HD)
        second = pltpu.roll(x[:, 1].reshape(-1, 2 * HD), HD, 1)
        even = jnp.where(low, first, second).astype(jnp.bfloat16)
        odd = jnp.where(low, second, first).astype(jnp.bfloat16)
        return even, odd

    def project_q(j, c):
        columns = pl.ds(pl.multiple_of(j * 256, 256), 256)
        query = dot(xall[pl.ds(0, rows), :], wq[:, columns])
        for p in range(2):
            even, odd = split(query[:, p * 128 : (p + 1) * 128], 1)
            qsend[4 * j + 2 * p] = even
            qsend[4 * j + 2 * p + 1] = odd
        return c

    loads[0].wait()
    loads[1].wait()
    lax.fori_loop(0, width // 256, project_q, 0)

    pl.semaphore_wait(barrier, nview + ntok - 2)

    def view_copy(i, name):
        to = peer(i, 1)
        target = (to, tok)

        def remote(src, dst, send, recv, at):
            return pltpu.make_async_remote_copy(
                src_ref=src, dst_ref=dst, send_sem=send.at[at], recv_sem=recv.at[at],
                device_id=target, device_id_type=MESH,
            )

        own = pl.ds((nview + view) * 2 * nblk, 2 * nblk)
        if name == "c":
            return remote(csend.at[to], condkv.at[tok, view], c_ss, c_rs, i)
        if name == "l":
            return remote(lsend, lists_v.at[view], l_ss, l_rs, i)
        if name == "q":
            return remote(qsend.at[to], qrecv.at[view], q_ss, q_rs, i)
        return remote(kvsend.at[to], pool.at[own], kv_ss, kv_rs, i)

    def start(*names, lo=1, hi=nview):
        def body(i, c):
            for name in names:
                view_copy(i, name).start()
            return c

        lax.fori_loop(lo, hi, body, 0)

    start("q", hi=1 + FIRST)
    for load in loads[2:]:
        load.wait()

    def project_kv(j, c):
        columns = pl.ds(pl.multiple_of(j * 256, 256), 256)
        keys = dot(xall[...], wk[:, columns])
        values = dot(xall[...], wv[:, columns])
        for p in range(2):
            head = 4 * j + 2 * p
            k = keys[:, p * 128 : (p + 1) * 128]
            v = values[:, p * 128 : (p + 1) * 128]
            for at, x in ((pl.ds(0, nblk), k), (pl.ds(nblk, nblk), v)):
                even, odd = split(x[:rows], nblk)
                kvsend[head, at] = even.reshape(nblk, BLK // 2, 2 * HD)
                kvsend[head + 1, at] = odd.reshape(nblk, BLK // 2, 2 * HD)
            k, v = k[rows:], pltpu.roll(v[rows:], HD, 1)
            csend[head] = jnp.where(low, k, v).astype(jnp.bfloat16)
            csend[head + 1] = jnp.where(low, v, k).astype(jnp.bfloat16)
        return c

    lax.fori_loop(0, width // 256, project_kv, 0)
    raw = lraw[...]
    entry_view, entry_block = raw[:, 0, :], raw[:, 1, :] - (tok - 1) * nblk
    band, inner = entry_block // nblk, lax.rem(entry_block, nblk)
    place = (band * nview + entry_view) * 2 * nblk + inner
    place = jnp.where(entry_view >= 0, place, unused)
    place = jnp.clip(place, 0, unused)
    lsend[...] = jnp.zeros((8, 128), jnp.int32)
    lsend[pl.ds(0, nblk), pl.ds(0, most)] = place
    start("c", "l")
    start("q", lo=1 + FIRST)
    start("kv")
    condkv[tok, view] = csend[view]
    lists_v[view] = lsend[...]
    qrecv[view] = qsend[view]
    pool[pl.ds((nview + view) * 2 * nblk, 2 * nblk)] = kvsend[view]

    def wait_view(name, start_i=1):
        def body(i, c):
            view_copy(i, name).wait_recv()
            return c

        lax.fori_loop(start_i, nview, body, 0)

    wait_view("c")

    def tok_copy(i):
        return pltpu.make_async_remote_copy(
            src_ref=condkv.at[tok], dst_ref=condkv.at[tok],
            send_sem=g_ss.at[i], recv_sem=g_rs.at[i],
            device_id=(view, lax.rem(tok + i, ntok)), device_id_type=MESH,
        )

    def start_tok(i, c):
        tok_copy(i).start()
        return c

    def wait_tok(i, c):
        tok_copy(i).wait_recv()
        return c

    lax.fori_loop(1, ntok, start_tok, 0)
    lax.fori_loop(1, ntok, wait_tok, 0)

    parity = lax.rem(view, 2)
    lane = lax.broadcasted_iota(jnp.int32, (1, 2 * HD), 1)
    khalf = (lane // HD) == parity
    kf = jnp.where(khalf, 1.0, 0.0)
    krow = kf.astype(jnp.bfloat16)
    vrow = (1.0 - kf).astype(jnp.bfloat16)
    count = ntok * nview * crows

    spare = condkv[0, pl.ds(0, BLK // crows)].reshape(BLK, 2 * HD).astype(jnp.float32)
    pool[unused] = jnp.where(
        khalf, spare[: BLK // 2], pltpu.roll(spare[BLK // 2 :], HD, 1)
    ).astype(jnp.bfloat16)
    pool[unused + nblk] = jnp.zeros((BLK // 2, 2 * HD), jnp.bfloat16)
    vcond[...] = condkv[...].reshape(count, 2 * HD) * vrow + krow

    def forward(i, direction):
        owner = peer(i, -1) * 2 * nblk
        step = 1 if direction == 0 else ntok - 1
        return pltpu.make_async_remote_copy(
            src_ref=pool.at[pl.ds(nview * 2 * nblk + owner, 2 * nblk)],
            dst_ref=pool.at[pl.ds(2 * direction * nview * 2 * nblk + owner, 2 * nblk)],
            send_sem=f_ss.at[direction, i], recv_sem=f_rs.at[direction, i],
            device_id=(view, lax.rem(tok + step, ntok)), device_id_type=MESH,
        )

    forward(0, 0).start()
    forward(0, 1).start()

    def pass_on(i):
        view_copy(i, "kv").wait_recv()
        forward(i, 0).start()
        forward(i, 1).start()

    def cond_step(i, c):
        @pl.when(i > 0)
        def _():
            view_copy(i, "q").wait_recv()

        packed = qrecv[peer(i, -1)].astype(jnp.float32)
        rolled = pltpu.roll(packed, HD, 1)
        first = [
            jnp.where(khalf, packed, 0.0).astype(jnp.bfloat16),
            jnp.where(khalf, rolled, 0.0).astype(jnp.bfloat16),
        ]
        other = [
            jnp.where(khalf, 0.0, rolled).astype(jnp.bfloat16),
            jnp.where(khalf, 0.0, packed).astype(jnp.bfloat16),
        ]
        ck = condkv[...].reshape(count, 2 * HD)
        scores = [dot_t(first[part], ck) for part in range(2)]
        for part in range(2):
            peak = jnp.max(scores[part], axis=1, keepdims=True)
            weights = jnp.exp2((scores[part] - peak) * scale).astype(jnp.bfloat16)
            total = dot(weights, vcond[...])
            peak = jnp.broadcast_to(peak, (half, 2 * HD))
            for b in range(nblk // 2):
                at = slice(b * BLK, (b + 1) * BLK)
                to = part * (nblk // 2) + b
                qstk[i, to, pl.ds(0, BLK)] = first[part][at]
                qstk[i, to, pl.ds(BLK, BLK)] = other[part][at]
                turned = total[at].T
                acc_t[i, to, pl.ds(0, HD)] = jnp.where(parity == 0, turned[HD:], turned[:HD])
                acc_t[i, to, pl.ds(HD, 8)] = jnp.where(
                    parity == 0, turned[:8], turned[HD : HD + 8]
                )
                peak_t[i, to] = peak[at].T[:8]

        @pl.when(i > LAG)
        def _():
            pass_on(i - LAG)

        return c

    lax.fori_loop(0, nview, cond_step, 0)

    def rest(i, c):
        pass_on(i)
        return c

    lax.fori_loop(nview - LAG, nview, rest, 0)
    wait_view("l")
    to_smem = pltpu.make_async_copy(lists_v, lists_s, smem_sem)
    to_smem.start()
    to_smem.wait()

    def wait_forward(i, c):
        forward(i, 0).wait_recv()
        forward(i, 1).wait_recv()
        return c

    lax.fori_loop(0, nview, wait_forward, 0)

    def o_copy(i):
        return pltpu.make_async_remote_copy(
            src_ref=osend.at[i], dst_ref=orecv.at[view],
            send_sem=o_ss.at[i], recv_sem=o_rs.at[i],
            device_id=(peer(i, -1), tok), device_id_type=MESH,
        )

    half_lane = lane < HD

    def epi_step(j, c):
        steps = [lax.rem(VPS * j + a + 1, nview) for a in range(VPS)]
        work = [(i, peer(i, -1), b) for i in steps for b in range(nblk)]
        scores, parts = [], []
        for i, owner, b in work:
            keys = jnp.concatenate([pool[lists_s[owner, b, s]] for s in range(most)], axis=0)
            scores.append(dot_t(keys, qstk[i, b]))
        for (i, owner, b), score in zip(work, scores):
            before = peak_t[i, b][:1]
            peak = jnp.max(score, axis=0, keepdims=True)
            peak = jnp.maximum(jnp.maximum(peak[:, :BLK], peak[:, BLK:]), before)
            weights = jnp.exp2((score - jnp.concatenate([peak, peak], axis=1)) * scale)
            weights = weights.astype(jnp.bfloat16)
            fade = jnp.exp2((before - peak) * scale)
            entries = [lists_s[owner, b, s] for s in range(most)]
            used = [jnp.where(entry < unused, 1.0, 0.0) for entry in entries]
            values = jnp.concatenate([pool[entry + nblk] for entry in entries], axis=0)
            sums = jnp.concatenate(
                [
                    jnp.broadcast_to(jnp.where(half_lane, used[s], used[s + 1]), (16, 2 * HD))
                    for s in range(0, most, 2)
                ],
                axis=1,
            ).astype(jnp.bfloat16)
            both = dot(jnp.concatenate([values.T, sums], axis=0), weights)
            top, ones = both[: 2 * HD], both[2 * HD :]
            part = jnp.where(
                parity == 0,
                top[:HD, :BLK] + top[HD:, BLK:],
                top[HD:, :BLK] + top[:HD, BLK:],
            )
            total = ones[:1, :BLK] + ones[:1, BLK:] + acc_t[i, b, pl.ds(HD, 8)][:1] * fade
            parts.append((part + acc_t[i, b, pl.ds(0, HD)] * fade) / total)
        for a, i in enumerate(steps):
            mine = parts[a * nblk : (a + 1) * nblk]
            for b in range(nblk // 2):
                pair = jnp.concatenate([mine[b], mine[b + nblk // 2]], axis=0)
                osend[i, pl.ds(b * BLK, BLK)] = pair.T.astype(jnp.bfloat16)
            if a < VPS - 1:
                o_copy(i).start()
            else:

                @pl.when(i > 0)
                def _():
                    o_copy(i).start()

                @pl.when(i == 0)
                def _():
                    orecv[view] = osend[i]

        return c

    lax.fori_loop(0, nview // VPS, epi_step, 0)

    def wait_o(i, c):
        o_copy(i).wait_recv()
        return c

    lax.fori_loop(1, nview, wait_o, 0)

    for j in range(nview // 2):
        even = orecv[2 * j].astype(jnp.float32)
        odd = orecv[2 * j + 1].astype(jnp.float32)
        at = pl.ds(j * 128, 128)
        att[pl.ds(0, half), at] = jnp.where(low, even, pltpu.roll(odd, HD, 1)).astype(jnp.bfloat16)
        att[pl.ds(half, half), at] = jnp.where(low, pltpu.roll(even, HD, 1), odd).astype(
            jnp.bfloat16
        )

    store = pltpu.make_async_copy(att, out_hbm, out_sem)
    store.start()

    def wait_sends(i, c):
        for name in ("c", "l", "q", "kv"):
            view_copy(i, name).wait_send()
        o_copy(i).wait_send()
        return c

    def wait_tok_sends(i, c):
        tok_copy(i).wait_send()
        return c

    def wait_forward_sends(i, c):
        forward(i, 0).wait_send()
        forward(i, 1).wait_send()
        return c

    lax.fori_loop(1, nview, wait_sends, 0)
    lax.fori_loop(1, ntok, wait_tok_sends, 0)
    lax.fori_loop(0, nview, wait_forward_sends, 0)
    store.wait()


def local(x_target, cond_x, w_query, w_key, w_value, w_out, epi_lists):
    nview = lax.axis_size("view")
    ntok = lax.axis_size("tok")
    rows, width = x_target.shape[1:]
    crows = cond_x.shape[0]
    most = epi_lists.shape[2]
    nblk = rows // BLK
    lists = jnp.transpose(epi_lists[0], (0, 2, 1))
    bf, f32 = jnp.bfloat16, jnp.float32
    half = rows // 2
    dma = pltpu.SemaphoreType.DMA
    scratch = [
        pltpu.VMEM((rows + crows, width), bf),
        pltpu.VMEM((width, width), bf),
        pltpu.VMEM((width, width), bf),
        pltpu.VMEM((width, width), bf),
        pltpu.VMEM((nview, half, 128), bf),
        pltpu.VMEM((nview, 2 * nblk, BLK // 2, 128), bf),
        pltpu.VMEM((nview, crows, 128), bf),
        pltpu.VMEM((nblk, 2, most), jnp.int32),
        pltpu.VMEM((8, 128), jnp.int32),
        pltpu.VMEM((nview, half, 128), bf),
        pltpu.VMEM((3 * nview * 2 * nblk + nblk + 1, BLK // 2, 128), bf),
        pltpu.VMEM((ntok, nview, crows, 128), bf),
        pltpu.VMEM((nview, 8, 128), jnp.int32),
        pltpu.SMEM((nview, 8, 128), jnp.int32),
        pltpu.VMEM((ntok * nview * crows, 128), bf),
        pltpu.VMEM((nview, nblk, 2 * BLK, 128), bf),
        pltpu.VMEM((nview, nblk, HD + 8, BLK), f32),
        pltpu.VMEM((nview, nblk, 8, BLK), f32),
        pltpu.VMEM((nview, half, 128), bf),
        pltpu.VMEM((nview, half, 128), bf),
        pltpu.VMEM((rows, width), bf),
        dma((6,)),
        dma((nview,)), dma((nview,)),
        dma((nview,)), dma((nview,)),
        *[dma((nview,)) for _ in range(4)],
        dma((ntok,)), dma((ntok,)),
        dma((2, nview)), dma((2, nview)),
        dma((nview,)), dma((nview,)),
        dma, dma,
    ]
    attended = pl.pallas_call(
        functools.partial(kernel, nview, ntok, math.isqrt(nview), rows, crows, most),
        out_shape=jax.ShapeDtypeStruct((rows, width), bf),
        in_specs=[pl.BlockSpec(memory_space=pl.ANY)] * 6,
        out_specs=pl.BlockSpec(memory_space=pl.ANY),
        scratch_shapes=scratch,
        compiler_params=pltpu.CompilerParams(
            collective_id=0, has_side_effects=True, vmem_limit_bytes=60 * 1024 * 1024
        ),
    )(x_target[0], cond_x, w_query, w_key, w_value, lists)
    return dot(attended, w_out).astype(bf)[None]


def solution(mesh):
    placed = (
        P("view", "tok", None),
        P(("view", "tok"), None),
        P(),
        P(),
        P(),
        P(),
        P("view", "tok", None, None),
    )
    return jax.shard_map(
        local, mesh=mesh, in_specs=placed, out_specs=P("view", "tok", None), check_vma=False
    )
```

```python
import functools
import math

import jax
import jax.numpy as jnp
from jax import lax
from jax.experimental import pallas as pl
from jax.experimental.pallas import tpu as pltpu
from jax.sharding import PartitionSpec as P

HD = 64
BLK = 128
MESH = pl.DeviceIdType.MESH
LAG = 1
FIRST = 7
VPS = 4


def dot(a, b):
    return jnp.dot(a, b, preferred_element_type=jnp.float32)


def dot_t(a, b):
    return lax.dot_general(a, b, (((1,), (1,)), ((), ())), preferred_element_type=jnp.float32)


def kernel(
    nview, ntok, side, rows, crows, most,
    x_hbm, cond_hbm, wq_hbm, wk_hbm, wv_hbm, lists_hbm,
    out_hbm,
    xall, wq, wk, wv,
    qsend, kvsend, csend, lraw, lsend,
    qrecv, pool, condkv, lists_v, lists_s,
    vcond, qstk, acc_t, peak_t, osend, orecv, att,
    load_sem, q_ss, q_rs, kv_ss, kv_rs, c_ss, c_rs, l_ss, l_rs, g_ss, g_rs, f_ss, f_rs, o_ss, o_rs, smem_sem, out_sem,
):
    view = lax.axis_index("view")
    tok = lax.axis_index("tok")
    width = nview * HD
    half = rows // 2
    nblk = rows // BLK
    scale = math.log2(math.e) * HD ** -0.5
    unused = 3 * nview * 2 * nblk

    loads = [
        pltpu.make_async_copy(x_hbm, xall.at[pl.ds(0, rows)], load_sem.at[0]),
        pltpu.make_async_copy(wq_hbm, wq, load_sem.at[1]),
        pltpu.make_async_copy(cond_hbm, xall.at[pl.ds(rows, crows)], load_sem.at[2]),
        pltpu.make_async_copy(wk_hbm, wk, load_sem.at[3]),
        pltpu.make_async_copy(wv_hbm, wv, load_sem.at[4]),
        pltpu.make_async_copy(lists_hbm, lraw, load_sem.at[5]),
    ]
    for load in loads:
        load.start()

    barrier = pltpu.get_barrier_semaphore()

    def peer(i, sign):
        dx, dy = lax.rem(i, side), lax.rem(i + i // side, side)
        x = lax.rem(view // side + sign * dx + side, side)
        y = lax.rem(lax.rem(view, side) + sign * dy + side, side)
        return x * side + y

    def greet_view(i, c):
        pl.semaphore_signal(barrier, inc=1, device_id=(peer(i, 1), tok), device_id_type=MESH)
        return c

    def greet_tok(i, c):
        pl.semaphore_signal(
            barrier, inc=1, device_id=(view, lax.rem(tok + i, ntok)), device_id_type=MESH
        )
        return c

    lax.fori_loop(1, nview, greet_view, 0)
    lax.fori_loop(1, ntok, greet_tok, 0)

    low = lax.broadcasted_iota(jnp.int32, (1, 2 * HD), 1) < HD

    def split(x, count):
        x = x.reshape(count, 2, -1, 2 * HD)
        first = x[:, 0].reshape(-1, 2 * HD)
        second = pltpu.roll(x[:, 1].reshape(-1, 2 * HD), HD, 1)
        even = jnp.where(low, first, second).astype(jnp.bfloat16)
        odd = jnp.where(low, second, first).astype(jnp.bfloat16)
        return even, odd

    def project_q(j, c):
        columns = pl.ds(pl.multiple_of(j * 256, 256), 256)
        query = dot(xall[pl.ds(0, rows), :], wq[:, columns])
        for p in range(2):
            even, odd = split(query[:, p * 128 : (p + 1) * 128], 1)
            qsend[4 * j + 2 * p] = even
            qsend[4 * j + 2 * p + 1] = odd
        return c

    loads[0].wait()
    loads[1].wait()
    lax.fori_loop(0, width // 256, project_q, 0)

    pl.semaphore_wait(barrier, nview + ntok - 2)

    def view_copy(i, name):
        to = peer(i, 1)
        target = (to, tok)

        def remote(src, dst, send, recv, at):
            return pltpu.make_async_remote_copy(
                src_ref=src, dst_ref=dst, send_sem=send.at[at], recv_sem=recv.at[at],
                device_id=target, device_id_type=MESH,
            )

        own = pl.ds((nview + view) * 2 * nblk, 2 * nblk)
        if name == "c":
            return remote(csend.at[to], condkv.at[tok, view], c_ss, c_rs, i)
        if name == "l":
            return remote(lsend, lists_v.at[view], l_ss, l_rs, i)
        if name == "q":
            return remote(qsend.at[to], qrecv.at[view], q_ss, q_rs, i)
        return remote(kvsend.at[to], pool.at[own], kv_ss, kv_rs, i)

    def start(*names, lo=1, hi=nview):
        def body(i, c):
            for name in names:
                view_copy(i, name).start()
            return c

        lax.fori_loop(lo, hi, body, 0)

    start("q", hi=1 + FIRST)
    for load in loads[2:]:
        load.wait()

    def project_kv(j, c):
        columns = pl.ds(pl.multiple_of(j * 256, 256), 256)
        keys = dot(xall[...], wk[:, columns])
        values = dot(xall[...], wv[:, columns])
        for p in range(2):
            head = 4 * j + 2 * p
            k = keys[:, p * 128 : (p + 1) * 128]
            v = values[:, p * 128 : (p + 1) * 128]
            for at, x in ((pl.ds(0, nblk), k), (pl.ds(nblk, nblk), v)):
                even, odd = split(x[:rows], nblk)
                kvsend[head, at] = even.reshape(nblk, BLK // 2, 2 * HD)
                kvsend[head + 1, at] = odd.reshape(nblk, BLK // 2, 2 * HD)
            k, v = k[rows:], pltpu.roll(v[rows:], HD, 1)
            csend[head] = jnp.where(low, k, v).astype(jnp.bfloat16)
            csend[head + 1] = jnp.where(low, v, k).astype(jnp.bfloat16)
        return c

    lax.fori_loop(0, width // 256, project_kv, 0)
    raw = lraw[...]
    entry_view, entry_block = raw[:, 0, :], raw[:, 1, :] - (tok - 1) * nblk
    band, inner = entry_block // nblk, lax.rem(entry_block, nblk)
    place = (band * nview + entry_view) * 2 * nblk + inner
    place = jnp.where(entry_view >= 0, place, unused)
    place = jnp.clip(place, 0, unused)
    lsend[...] = jnp.zeros((8, 128), jnp.int32)
    lsend[pl.ds(0, nblk), pl.ds(0, most)] = place
    start("c", "l")
    start("q", lo=1 + FIRST)
    start("kv")
    condkv[tok, view] = csend[view]
    lists_v[view] = lsend[...]
    qrecv[view] = qsend[view]
    pool[pl.ds((nview + view) * 2 * nblk, 2 * nblk)] = kvsend[view]

    def wait_view(name, start_i=1):
        def body(i, c):
            view_copy(i, name).wait_recv()
            return c

        lax.fori_loop(start_i, nview, body, 0)

    wait_view("c")

    def tok_copy(i):
        return pltpu.make_async_remote_copy(
            src_ref=condkv.at[tok], dst_ref=condkv.at[tok],
            send_sem=g_ss.at[i], recv_sem=g_rs.at[i],
            device_id=(view, lax.rem(tok + i, ntok)), device_id_type=MESH,
        )

    def start_tok(i, c):
        tok_copy(i).start()
        return c

    def wait_tok(i, c):
        tok_copy(i).wait_recv()
        return c

    lax.fori_loop(1, ntok, start_tok, 0)
    lax.fori_loop(1, ntok, wait_tok, 0)

    parity = lax.rem(view, 2)
    lane = lax.broadcasted_iota(jnp.int32, (1, 2 * HD), 1)
    khalf = (lane // HD) == parity
    kf = jnp.where(khalf, 1.0, 0.0)
    krow = kf.astype(jnp.bfloat16)
    vrow = (1.0 - kf).astype(jnp.bfloat16)
    count = ntok * nview * crows

    spare = condkv[0, pl.ds(0, BLK // crows)].reshape(BLK, 2 * HD).astype(jnp.float32)
    pool[unused] = jnp.where(
        khalf, spare[: BLK // 2], pltpu.roll(spare[BLK // 2 :], HD, 1)
    ).astype(jnp.bfloat16)
    pool[unused + nblk] = jnp.zeros((BLK // 2, 2 * HD), jnp.bfloat16)
    vcond[...] = condkv[...].reshape(count, 2 * HD) * vrow + krow

    def forward(i, direction):
        owner = peer(i, -1) * 2 * nblk
        step = 1 if direction == 0 else ntok - 1
        return pltpu.make_async_remote_copy(
            src_ref=pool.at[pl.ds(nview * 2 * nblk + owner, 2 * nblk)],
            dst_ref=pool.at[pl.ds(2 * direction * nview * 2 * nblk + owner, 2 * nblk)],
            send_sem=f_ss.at[direction, i], recv_sem=f_rs.at[direction, i],
            device_id=(view, lax.rem(tok + step, ntok)), device_id_type=MESH,
        )

    forward(0, 0).start()
    forward(0, 1).start()

    def pass_on(i):
        view_copy(i, "kv").wait_recv()
        forward(i, 0).start()
        forward(i, 1).start()

    def cond_step(i, c):
        @pl.when(i > 0)
        def _():
            view_copy(i, "q").wait_recv()

        packed = qrecv[peer(i, -1)].astype(jnp.float32)
        rolled = pltpu.roll(packed, HD, 1)
        first = [
            jnp.where(khalf, packed, 0.0).astype(jnp.bfloat16),
            jnp.where(khalf, rolled, 0.0).astype(jnp.bfloat16),
        ]
        other = [
            jnp.where(khalf, 0.0, rolled).astype(jnp.bfloat16),
            jnp.where(khalf, 0.0, packed).astype(jnp.bfloat16),
        ]
        ck = condkv[...].reshape(count, 2 * HD)
        scores = [dot_t(first[part], ck) for part in range(2)]
        for part in range(2):
            peak = jnp.max(scores[part], axis=1, keepdims=True)
            weights = jnp.exp2((scores[part] - peak) * scale).astype(jnp.bfloat16)
            total = dot(weights, vcond[...])
            peak = jnp.broadcast_to(peak, (half, 2 * HD))
            for b in range(nblk // 2):
                at = slice(b * BLK, (b + 1) * BLK)
                to = part * (nblk // 2) + b
                qstk[i, to, pl.ds(0, BLK)] = first[part][at]
                qstk[i, to, pl.ds(BLK, BLK)] = other[part][at]
                turned = total[at].T
                acc_t[i, to, pl.ds(0, HD)] = jnp.where(parity == 0, turned[HD:], turned[:HD])
                acc_t[i, to, pl.ds(HD, 8)] = jnp.where(
                    parity == 0, turned[:8], turned[HD : HD + 8]
                )
                peak_t[i, to] = peak[at].T[:8]

        @pl.when(i > LAG)
        def _():
            pass_on(i - LAG)

        return c

    lax.fori_loop(0, nview, cond_step, 0)

    def rest(i, c):
        pass_on(i)
        return c

    lax.fori_loop(nview - LAG, nview, rest, 0)
    wait_view("l")
    to_smem = pltpu.make_async_copy(lists_v, lists_s, smem_sem)
    to_smem.start()
    to_smem.wait()

    def wait_forward(i, c):
        forward(i, 0).wait_recv()
        forward(i, 1).wait_recv()
        return c

    lax.fori_loop(0, nview, wait_forward, 0)

    def o_copy(i):
        return pltpu.make_async_remote_copy(
            src_ref=osend.at[i], dst_ref=orecv.at[view],
            send_sem=o_ss.at[i], recv_sem=o_rs.at[i],
            device_id=(peer(i, -1), tok), device_id_type=MESH,
        )

    half_lane = lane < HD

    def epi_step(j, c):
        steps = [lax.rem(VPS * j + a + 1, nview) for a in range(VPS)]
        work = [(i, peer(i, -1), b) for i in steps for b in range(nblk)]
        scores, parts = [], []
        for i, owner, b in work:
            keys = jnp.concatenate([pool[lists_s[owner, b, s]] for s in range(most)], axis=0)
            scores.append(dot_t(keys, qstk[i, b]))
        for (i, owner, b), score in zip(work, scores):
            before = peak_t[i, b][:1]
            peak = jnp.max(score, axis=0, keepdims=True)
            peak = jnp.maximum(jnp.maximum(peak[:, :BLK], peak[:, BLK:]), before)
            weights = jnp.exp2((score - jnp.concatenate([peak, peak], axis=1)) * scale)
            weights = weights.astype(jnp.bfloat16)
            fade = jnp.exp2((before - peak) * scale)
            entries = [lists_s[owner, b, s] for s in range(most)]
            used = [jnp.where(entry < unused, 1.0, 0.0) for entry in entries]
            values = jnp.concatenate([pool[entry + nblk] for entry in entries], axis=0)
            sums = jnp.concatenate(
                [
                    jnp.broadcast_to(jnp.where(half_lane, used[s], used[s + 1]), (16, 2 * HD))
                    for s in range(0, most, 2)
                ],
                axis=1,
            ).astype(jnp.bfloat16)
            both = dot(jnp.concatenate([values.T, sums], axis=0), weights)
            top, ones = both[: 2 * HD], both[2 * HD :]
            part = jnp.where(
                parity == 0,
                top[:HD, :BLK] + top[HD:, BLK:],
                top[HD:, :BLK] + top[:HD, BLK:],
            )
            total = ones[:1, :BLK] + ones[:1, BLK:] + acc_t[i, b, pl.ds(HD, 8)][:1] * fade
            parts.append((part + acc_t[i, b, pl.ds(0, HD)] * fade) / total)
        for a, i in enumerate(steps):
            mine = parts[a * nblk : (a + 1) * nblk]
            for b in range(nblk // 2):
                pair = jnp.concatenate([mine[b], mine[b + nblk // 2]], axis=0)
                osend[i, pl.ds(b * BLK, BLK)] = pair.T.astype(jnp.bfloat16)
            if a < VPS - 1:
                o_copy(i).start()
            else:

                @pl.when(i > 0)
                def _():
                    o_copy(i).start()

                @pl.when(i == 0)
                def _():
                    orecv[view] = osend[i]

        return c

    lax.fori_loop(0, nview // VPS, epi_step, 0)

    def wait_o(i, c):
        o_copy(i).wait_recv()
        return c

    lax.fori_loop(1, nview, wait_o, 0)

    for j in range(nview // 2):
        even = orecv[2 * j].astype(jnp.float32)
        odd = orecv[2 * j + 1].astype(jnp.float32)
        at = pl.ds(j * 128, 128)
        att[pl.ds(0, half), at] = jnp.where(low, even, pltpu.roll(odd, HD, 1)).astype(jnp.bfloat16)
        att[pl.ds(half, half), at] = jnp.where(low, pltpu.roll(even, HD, 1), odd).astype(
            jnp.bfloat16
        )

    store = pltpu.make_async_copy(att, out_hbm, out_sem)
    store.start()

    def wait_sends(i, c):
        for name in ("c", "l", "q", "kv"):
            view_copy(i, name).wait_send()
        o_copy(i).wait_send()
        return c

    def wait_tok_sends(i, c):
        tok_copy(i).wait_send()
        return c

    def wait_forward_sends(i, c):
        forward(i, 0).wait_send()
        forward(i, 1).wait_send()
        return c

    lax.fori_loop(1, nview, wait_sends, 0)
    lax.fori_loop(1, ntok, wait_tok_sends, 0)
    lax.fori_loop(0, nview, wait_forward_sends, 0)
    store.wait()


def local(x_target, cond_x, w_query, w_key, w_value, w_out, epi_lists):
    nview = lax.axis_size("view")
    ntok = lax.axis_size("tok")
    rows, width = x_target.shape[1:]
    crows = cond_x.shape[0]
    most = epi_lists.shape[2]
    nblk = rows // BLK
    lists = jnp.transpose(epi_lists[0], (0, 2, 1))
    bf, f32 = jnp.bfloat16, jnp.float32
    half = rows // 2
    dma = pltpu.SemaphoreType.DMA
    scratch = [
        pltpu.VMEM((rows + crows, width), bf),
        pltpu.VMEM((width, width), bf),
        pltpu.VMEM((width, width), bf),
        pltpu.VMEM((width, width), bf),
        pltpu.VMEM((nview, half, 128), bf),
        pltpu.VMEM((nview, 2 * nblk, BLK // 2, 128), bf),
        pltpu.VMEM((nview, crows, 128), bf),
        pltpu.VMEM((nblk, 2, most), jnp.int32),
        pltpu.VMEM((8, 128), jnp.int32),
        pltpu.VMEM((nview, half, 128), bf),
        pltpu.VMEM((3 * nview * 2 * nblk + nblk + 1, BLK // 2, 128), bf),
        pltpu.VMEM((ntok, nview, crows, 128), bf),
        pltpu.VMEM((nview, 8, 128), jnp.int32),
        pltpu.SMEM((nview, 8, 128), jnp.int32),
        pltpu.VMEM((ntok * nview * crows, 128), bf),
        pltpu.VMEM((nview, nblk, 2 * BLK, 128), bf),
        pltpu.VMEM((nview, nblk, HD + 8, BLK), f32),
        pltpu.VMEM((nview, nblk, 8, BLK), f32),
        pltpu.VMEM((nview, half, 128), bf),
        pltpu.VMEM((nview, half, 128), bf),
        pltpu.VMEM((rows, width), bf),
        dma((6,)),
        dma((nview,)), dma((nview,)),
        dma((nview,)), dma((nview,)),
        *[dma((nview,)) for _ in range(4)],
        dma((ntok,)), dma((ntok,)),
        dma((2, nview)), dma((2, nview)),
        dma((nview,)), dma((nview,)),
        dma, dma,
    ]
    attended = pl.pallas_call(
        functools.partial(kernel, nview, ntok, math.isqrt(nview), rows, crows, most),
        out_shape=jax.ShapeDtypeStruct((rows, width), bf),
        in_specs=[pl.BlockSpec(memory_space=pl.ANY)] * 6,
        out_specs=pl.BlockSpec(memory_space=pl.ANY),
        scratch_shapes=scratch,
        compiler_params=pltpu.CompilerParams(
            collective_id=0, has_side_effects=True, vmem_limit_bytes=60 * 1024 * 1024
        ),
    )(x_target[0], cond_x, w_query, w_key, w_value, lists)
    return dot(attended, w_out).astype(bf)[None]


def solution(mesh):
    placed = (
        P("view", "tok", None),
        P(("view", "tok"), None),
        P(),
        P(),
        P(),
        P(),
        P("view", "tok", None, None),
    )
    return jax.shard_map(
        local, mesh=mesh, in_specs=placed, out_specs=P("view", "tok", None), check_vma=False
    )
```

```python
import functools
import math

import jax
import jax.numpy as jnp
from jax import lax
from jax.experimental import pallas as pl
from jax.experimental.pallas import tpu as pltpu
from jax.sharding import PartitionSpec as P

HD = 64
BLK = 128
MESH = pl.DeviceIdType.MESH
LAG = 1
FIRST = 5
VPS = 4


def dot(a, b):
    return jnp.dot(a, b, preferred_element_type=jnp.float32)


def dot_t(a, b):
    return lax.dot_general(a, b, (((1,), (1,)), ((), ())), preferred_element_type=jnp.float32)


def kernel(
    nview, ntok, side, rows, crows, most,
    x_hbm, cond_hbm, wq_hbm, wk_hbm, wv_hbm, lists_hbm,
    out_hbm,
    xall, wq, wk, wv,
    qsend, kvsend, csend, lraw, lsend,
    qrecv, pool, condkv, lists_v, lists_s,
    vcond, qstk, acc_t, peak_t, osend, orecv, att,
    load_sem, q_ss, q_rs, kv_ss, kv_rs, c_ss, c_rs, l_ss, l_rs, g_ss, g_rs, f_ss, f_rs, o_ss, o_rs, smem_sem, out_sem,
):
    view = lax.axis_index("view")
    tok = lax.axis_index("tok")
    width = nview * HD
    half = rows // 2
    nblk = rows // BLK
    scale = math.log2(math.e) * HD ** -0.5
    unused = 3 * nview * 2 * nblk

    loads = [
        pltpu.make_async_copy(x_hbm, xall.at[pl.ds(0, rows)], load_sem.at[0]),
        pltpu.make_async_copy(wq_hbm, wq, load_sem.at[1]),
        pltpu.make_async_copy(cond_hbm, xall.at[pl.ds(rows, crows)], load_sem.at[2]),
        pltpu.make_async_copy(wk_hbm, wk, load_sem.at[3]),
        pltpu.make_async_copy(wv_hbm, wv, load_sem.at[4]),
        pltpu.make_async_copy(lists_hbm, lraw, load_sem.at[5]),
    ]
    for load in loads:
        load.start()

    barrier = pltpu.get_barrier_semaphore()

    def peer(i, sign):
        dx, dy = lax.rem(i, side), lax.rem(i + i // side, side)
        x = lax.rem(view // side + sign * dx + side, side)
        y = lax.rem(lax.rem(view, side) + sign * dy + side, side)
        return x * side + y

    def greet_view(i, c):
        pl.semaphore_signal(barrier, inc=1, device_id=(peer(i, 1), tok), device_id_type=MESH)
        return c

    def greet_tok(i, c):
        pl.semaphore_signal(
            barrier, inc=1, device_id=(view, lax.rem(tok + i, ntok)), device_id_type=MESH
        )
        return c

    lax.fori_loop(1, nview, greet_view, 0)
    lax.fori_loop(1, ntok, greet_tok, 0)

    low = lax.broadcasted_iota(jnp.int32, (1, 2 * HD), 1) < HD

    def split(x, count):
        x = x.reshape(count, 2, -1, 2 * HD)
        first = x[:, 0].reshape(-1, 2 * HD)
        second = pltpu.roll(x[:, 1].reshape(-1, 2 * HD), HD, 1)
        even = jnp.where(low, first, second).astype(jnp.bfloat16)
        odd = jnp.where(low, second, first).astype(jnp.bfloat16)
        return even, odd

    def project_q(j, c):
        columns = pl.ds(pl.multiple_of(j * 256, 256), 256)
        query = dot(xall[pl.ds(0, rows), :], wq[:, columns])
        for p in range(2):
            even, odd = split(query[:, p * 128 : (p + 1) * 128], 1)
            qsend[4 * j + 2 * p] = even
            qsend[4 * j + 2 * p + 1] = odd
        return c

    loads[0].wait()
    loads[1].wait()
    lax.fori_loop(0, width // 256, project_q, 0)

    pl.semaphore_wait(barrier, nview + ntok - 2)

    def view_copy(i, name):
        to = peer(i, 1)
        target = (to, tok)

        def remote(src, dst, send, recv, at):
            return pltpu.make_async_remote_copy(
                src_ref=src, dst_ref=dst, send_sem=send.at[at], recv_sem=recv.at[at],
                device_id=target, device_id_type=MESH,
            )

        own = pl.ds((nview + view) * 2 * nblk, 2 * nblk)
        if name == "c":
            return remote(csend.at[to], condkv.at[tok, view], c_ss, c_rs, i)
        if name == "l":
            return remote(lsend, lists_v.at[view], l_ss, l_rs, i)
        if name == "q":
            return remote(qsend.at[to], qrecv.at[view], q_ss, q_rs, i)
        return remote(kvsend.at[to], pool.at[own], kv_ss, kv_rs, i)

    def start(*names, lo=1, hi=nview):
        def body(i, c):
            for name in names:
                view_copy(i, name).start()
            return c

        lax.fori_loop(lo, hi, body, 0)

    start("q", hi=1 + FIRST)
    for load in loads[2:]:
        load.wait()

    def project_kv(j, c):
        columns = pl.ds(pl.multiple_of(j * 256, 256), 256)
        keys = dot(xall[...], wk[:, columns])
        values = dot(xall[...], wv[:, columns])
        for p in range(2):
            head = 4 * j + 2 * p
            k = keys[:, p * 128 : (p + 1) * 128]
            v = values[:, p * 128 : (p + 1) * 128]
            for at, x in ((pl.ds(0, nblk), k), (pl.ds(nblk, nblk), v)):
                even, odd = split(x[:rows], nblk)
                kvsend[head, at] = even.reshape(nblk, BLK // 2, 2 * HD)
                kvsend[head + 1, at] = odd.reshape(nblk, BLK // 2, 2 * HD)
            k, v = k[rows:], pltpu.roll(v[rows:], HD, 1)
            csend[head] = jnp.where(low, k, v).astype(jnp.bfloat16)
            csend[head + 1] = jnp.where(low, v, k).astype(jnp.bfloat16)
        return c

    lax.fori_loop(0, width // 256, project_kv, 0)
    raw = lraw[...]
    entry_view, entry_block = raw[:, 0, :], raw[:, 1, :] - (tok - 1) * nblk
    band, inner = entry_block // nblk, lax.rem(entry_block, nblk)
    place = (band * nview + entry_view) * 2 * nblk + inner
    place = jnp.where(entry_view >= 0, place, unused)
    place = jnp.clip(place, 0, unused)
    lsend[...] = jnp.zeros((8, 128), jnp.int32)
    lsend[pl.ds(0, nblk), pl.ds(0, most)] = place
    start("c", "l")
    start("q", lo=1 + FIRST)
    start("kv")
    condkv[tok, view] = csend[view]
    lists_v[view] = lsend[...]
    qrecv[view] = qsend[view]
    pool[pl.ds((nview + view) * 2 * nblk, 2 * nblk)] = kvsend[view]

    def wait_view(name, start_i=1):
        def body(i, c):
            view_copy(i, name).wait_recv()
            return c

        lax.fori_loop(start_i, nview, body, 0)

    wait_view("c")

    def tok_copy(i):
        return pltpu.make_async_remote_copy(
            src_ref=condkv.at[tok], dst_ref=condkv.at[tok],
            send_sem=g_ss.at[i], recv_sem=g_rs.at[i],
            device_id=(view, lax.rem(tok + i, ntok)), device_id_type=MESH,
        )

    def start_tok(i, c):
        tok_copy(i).start()
        return c

    def wait_tok(i, c):
        tok_copy(i).wait_recv()
        return c

    lax.fori_loop(1, ntok, start_tok, 0)
    lax.fori_loop(1, ntok, wait_tok, 0)

    parity = lax.rem(view, 2)
    lane = lax.broadcasted_iota(jnp.int32, (1, 2 * HD), 1)
    khalf = (lane // HD) == parity
    kf = jnp.where(khalf, 1.0, 0.0)
    krow = kf.astype(jnp.bfloat16)
    vrow = (1.0 - kf).astype(jnp.bfloat16)
    count = ntok * nview * crows

    spare = condkv[0, pl.ds(0, BLK // crows)].reshape(BLK, 2 * HD).astype(jnp.float32)
    pool[unused] = jnp.where(
        khalf, spare[: BLK // 2], pltpu.roll(spare[BLK // 2 :], HD, 1)
    ).astype(jnp.bfloat16)
    pool[unused + nblk] = jnp.zeros((BLK // 2, 2 * HD), jnp.bfloat16)
    vcond[...] = condkv[...].reshape(count, 2 * HD) * vrow + krow

    def forward(i, direction):
        owner = peer(i, -1) * 2 * nblk
        step = 1 if direction == 0 else ntok - 1
        return pltpu.make_async_remote_copy(
            src_ref=pool.at[pl.ds(nview * 2 * nblk + owner, 2 * nblk)],
            dst_ref=pool.at[pl.ds(2 * direction * nview * 2 * nblk + owner, 2 * nblk)],
            send_sem=f_ss.at[direction, i], recv_sem=f_rs.at[direction, i],
            device_id=(view, lax.rem(tok + step, ntok)), device_id_type=MESH,
        )

    forward(0, 0).start()
    forward(0, 1).start()

    def pass_on(i):
        view_copy(i, "kv").wait_recv()
        forward(i, 0).start()
        forward(i, 1).start()

    def cond_step(i, c):
        @pl.when(i > 0)
        def _():
            view_copy(i, "q").wait_recv()

        packed = qrecv[peer(i, -1)].astype(jnp.float32)
        rolled = pltpu.roll(packed, HD, 1)
        first = [
            jnp.where(khalf, packed, 0.0).astype(jnp.bfloat16),
            jnp.where(khalf, rolled, 0.0).astype(jnp.bfloat16),
        ]
        other = [
            jnp.where(khalf, 0.0, rolled).astype(jnp.bfloat16),
            jnp.where(khalf, 0.0, packed).astype(jnp.bfloat16),
        ]
        ck = condkv[...].reshape(count, 2 * HD)
        scores = [dot_t(first[part], ck) for part in range(2)]
        for part in range(2):
            peak = jnp.max(scores[part], axis=1, keepdims=True)
            weights = jnp.exp2((scores[part] - peak) * scale).astype(jnp.bfloat16)
            total = dot(weights, vcond[...])
            peak = jnp.broadcast_to(peak, (half, 2 * HD))
            for b in range(nblk // 2):
                at = slice(b * BLK, (b + 1) * BLK)
                to = part * (nblk // 2) + b
                qstk[i, to, pl.ds(0, BLK)] = first[part][at]
                qstk[i, to, pl.ds(BLK, BLK)] = other[part][at]
                turned = total[at].T
                acc_t[i, to, pl.ds(0, HD)] = jnp.where(parity == 0, turned[HD:], turned[:HD])
                acc_t[i, to, pl.ds(HD, 8)] = jnp.where(
                    parity == 0, turned[:8], turned[HD : HD + 8]
                )
                peak_t[i, to] = peak[at].T[:8]

        @pl.when(i > LAG)
        def _():
            pass_on(i - LAG)

        return c

    lax.fori_loop(0, nview, cond_step, 0)

    def rest(i, c):
        pass_on(i)
        return c

    lax.fori_loop(nview - LAG, nview, rest, 0)
    wait_view("l")
    to_smem = pltpu.make_async_copy(lists_v, lists_s, smem_sem)
    to_smem.start()
    to_smem.wait()

    def wait_forward(i, c):
        forward(i, 0).wait_recv()
        forward(i, 1).wait_recv()
        return c

    lax.fori_loop(0, nview, wait_forward, 0)

    def o_copy(i):
        return pltpu.make_async_remote_copy(
            src_ref=osend.at[i], dst_ref=orecv.at[view],
            send_sem=o_ss.at[i], recv_sem=o_rs.at[i],
            device_id=(peer(i, -1), tok), device_id_type=MESH,
        )

    half_lane = lane < HD

    def epi_step(j, c):
        steps = [lax.rem(VPS * j + a + 1, nview) for a in range(VPS)]
        work = [(i, peer(i, -1), b) for i in steps for b in range(nblk)]
        scores, parts = [], []
        for i, owner, b in work:
            keys = jnp.concatenate([pool[lists_s[owner, b, s]] for s in range(most)], axis=0)
            scores.append(dot_t(keys, qstk[i, b]))
        for (i, owner, b), score in zip(work, scores):
            before = peak_t[i, b][:1]
            peak = jnp.max(score, axis=0, keepdims=True)
            peak = jnp.maximum(jnp.maximum(peak[:, :BLK], peak[:, BLK:]), before)
            weights = jnp.exp2((score - jnp.concatenate([peak, peak], axis=1)) * scale)
            weights = weights.astype(jnp.bfloat16)
            fade = jnp.exp2((before - peak) * scale)
            entries = [lists_s[owner, b, s] for s in range(most)]
            used = [jnp.where(entry < unused, 1.0, 0.0) for entry in entries]
            values = jnp.concatenate([pool[entry + nblk] for entry in entries], axis=0)
            sums = jnp.concatenate(
                [
                    jnp.broadcast_to(jnp.where(half_lane, used[s], used[s + 1]), (16, 2 * HD))
                    for s in range(0, most, 2)
                ],
                axis=1,
            ).astype(jnp.bfloat16)
            both = dot(jnp.concatenate([values.T, sums], axis=0), weights)
            top, ones = both[: 2 * HD], both[2 * HD :]
            part = jnp.where(
                parity == 0,
                top[:HD, :BLK] + top[HD:, BLK:],
                top[HD:, :BLK] + top[:HD, BLK:],
            )
            total = ones[:1, :BLK] + ones[:1, BLK:] + acc_t[i, b, pl.ds(HD, 8)][:1] * fade
            parts.append((part + acc_t[i, b, pl.ds(0, HD)] * fade) / total)
        for a, i in enumerate(steps):
            mine = parts[a * nblk : (a + 1) * nblk]
            for b in range(nblk // 2):
                pair = jnp.concatenate([mine[b], mine[b + nblk // 2]], axis=0)
                osend[i, pl.ds(b * BLK, BLK)] = pair.T.astype(jnp.bfloat16)
            if a < VPS - 1:
                o_copy(i).start()
            else:

                @pl.when(i > 0)
                def _():
                    o_copy(i).start()

                @pl.when(i == 0)
                def _():
                    orecv[view] = osend[i]

        return c

    lax.fori_loop(0, nview // VPS, epi_step, 0)

    def wait_o(i, c):
        o_copy(i).wait_recv()
        return c

    lax.fori_loop(1, nview, wait_o, 0)

    for j in range(nview // 2):
        even = orecv[2 * j].astype(jnp.float32)
        odd = orecv[2 * j + 1].astype(jnp.float32)
        at = pl.ds(j * 128, 128)
        att[pl.ds(0, half), at] = jnp.where(low, even, pltpu.roll(odd, HD, 1)).astype(jnp.bfloat16)
        att[pl.ds(half, half), at] = jnp.where(low, pltpu.roll(even, HD, 1), odd).astype(
            jnp.bfloat16
        )

    store = pltpu.make_async_copy(att, out_hbm, out_sem)
    store.start()

    def wait_sends(i, c):
        for name in ("c", "l", "q", "kv"):
            view_copy(i, name).wait_send()
        o_copy(i).wait_send()
        return c

    def wait_tok_sends(i, c):
        tok_copy(i).wait_send()
        return c

    def wait_forward_sends(i, c):
        forward(i, 0).wait_send()
        forward(i, 1).wait_send()
        return c

    lax.fori_loop(1, nview, wait_sends, 0)
    lax.fori_loop(1, ntok, wait_tok_sends, 0)
    lax.fori_loop(0, nview, wait_forward_sends, 0)
    store.wait()


def local(x_target, cond_x, w_query, w_key, w_value, w_out, epi_lists):
    nview = lax.axis_size("view")
    ntok = lax.axis_size("tok")
    rows, width = x_target.shape[1:]
    crows = cond_x.shape[0]
    most = epi_lists.shape[2]
    nblk = rows // BLK
    lists = jnp.transpose(epi_lists[0], (0, 2, 1))
    bf, f32 = jnp.bfloat16, jnp.float32
    half = rows // 2
    dma = pltpu.SemaphoreType.DMA
    scratch = [
        pltpu.VMEM((rows + crows, width), bf),
        pltpu.VMEM((width, width), bf),
        pltpu.VMEM((width, width), bf),
        pltpu.VMEM((width, width), bf),
        pltpu.VMEM((nview, half, 128), bf),
        pltpu.VMEM((nview, 2 * nblk, BLK // 2, 128), bf),
        pltpu.VMEM((nview, crows, 128), bf),
        pltpu.VMEM((nblk, 2, most), jnp.int32),
        pltpu.VMEM((8, 128), jnp.int32),
        pltpu.VMEM((nview, half, 128), bf),
        pltpu.VMEM((3 * nview * 2 * nblk + nblk + 1, BLK // 2, 128), bf),
        pltpu.VMEM((ntok, nview, crows, 128), bf),
        pltpu.VMEM((nview, 8, 128), jnp.int32),
        pltpu.SMEM((nview, 8, 128), jnp.int32),
        pltpu.VMEM((ntok * nview * crows, 128), bf),
        pltpu.VMEM((nview, nblk, 2 * BLK, 128), bf),
        pltpu.VMEM((nview, nblk, HD + 8, BLK), f32),
        pltpu.VMEM((nview, nblk, 8, BLK), f32),
        pltpu.VMEM((nview, half, 128), bf),
        pltpu.VMEM((nview, half, 128), bf),
        pltpu.VMEM((rows, width), bf),
        dma((6,)),
        dma((nview,)), dma((nview,)),
        dma((nview,)), dma((nview,)),
        *[dma((nview,)) for _ in range(4)],
        dma((ntok,)), dma((ntok,)),
        dma((2, nview)), dma((2, nview)),
        dma((nview,)), dma((nview,)),
        dma, dma,
    ]
    attended = pl.pallas_call(
        functools.partial(kernel, nview, ntok, math.isqrt(nview), rows, crows, most),
        out_shape=jax.ShapeDtypeStruct((rows, width), bf),
        in_specs=[pl.BlockSpec(memory_space=pl.ANY)] * 6,
        out_specs=pl.BlockSpec(memory_space=pl.ANY),
        scratch_shapes=scratch,
        compiler_params=pltpu.CompilerParams(
            collective_id=0, has_side_effects=True, vmem_limit_bytes=60 * 1024 * 1024
        ),
    )(x_target[0], cond_x, w_query, w_key, w_value, lists)
    return dot(attended, w_out).astype(bf)[None]


def solution(mesh):
    placed = (
        P("view", "tok", None),
        P(("view", "tok"), None),
        P(),
        P(),
        P(),
        P(),
        P("view", "tok", None, None),
    )
    return jax.shard_map(
        local, mesh=mesh, in_specs=placed, out_specs=P("view", "tok", None), check_vma=False
    )
```
